256 devices in a mesh: sq: 16 (over x, y), sk: 16 (over z, core).
Axes of the slice: x: 4, y: 4, z: 8, core: 2. Of those that a mesh axis runs over, the one named last changes fastest.
Arguments:
- video: bfloat16 [49152, 3072], P(('sq', 'sk')), may hold values from -6 to 6
- assign: int32 [49152], P(('sq', 'sk')), may hold values from 0 to 12287, as said below
- qkv_weight: bfloat16 [3072, 6144], P(None, 'sq'), may hold values from -0.109375 to 0.109375
- qk_gain: float32 [2, 128], replicated, may hold values from 1.5 to 2.5
- text_kv: bfloat16 [2, 256, 2048], P(None, None, 'sq')
- out_weight: bfloat16 [2048, 3072], P('sq'), may hold values from -0.125 to 0.125
Outputs:
- mixed: bfloat16 [49152, 3072], P(('sq', 'sk'))
The draws below stay inside these ranges and needn't reach their ends.
Inputs may be any that keep to these rules, and one draw needn't show every extreme that they name: `assign`: A video token of device index i*16+j of sq+sk merges into a token held by a device of the same j, merged token m being held by device m // 48. At most 24 of one device's tokens go to the tokens of one index of sq; in every draw each device sends exactly 24 to one of them. Merged tokens may have no video token.
All inputs are finite; a program needn't handle non-finite values.
Results may differ from the reference program's by a relative error of at most 0.01.
Values may be sent and summed in bfloat16 or wider, within the bound.
No kernel may reach another device: no remote copies, remote signals or barrier semaphores. Data moves between devices by JAX's collectives and lax.ppermute only.
A program may use at most 128 MiB of HBM per device.

```python
import math
import jax
import jax.numpy as jnp
from jax import lax

D = 3072
HEADS = 16
HD = 128
TEXT = 256
SRC_DEV = 192
MRG_DEV = 48
HEADS_DEV = 1
CAP = 24
SOURCE = 49152
MERGED = 12288
N_SQ = 16
N_SK = 16


def draw_assign(key, part):
    key = jax.random.fold_in(key, 11)
    key_score, key_full, key_first, key_second = jax.random.split(key, 4)
    devices_all = N_SQ * N_SK
    slot_total = N_SQ * CAP
    scores = jax.random.randint(key_score, (devices_all, slot_total), 0, 65536) * slot_total + jnp.arange(slot_total, dtype=jnp.int32)[None, :]
    full_peer = jax.random.randint(key_full, (devices_all, 1), 0, N_SQ)
    boosted = jnp.where(jnp.arange(slot_total, dtype=jnp.int32)[None, :] // CAP == full_peer, 268435456, 0)
    _, chosen = lax.top_k(scores + boosted, SRC_DEV)
    peer_index = chosen // CAP
    first_id = jax.random.randint(key_first, (devices_all, SRC_DEV), 0, MRG_DEV)
    second_id = jax.random.randint(key_second, (devices_all, SRC_DEV), 0, MRG_DEV)
    local_id = jnp.minimum(first_id, second_id)
    column_index = jnp.arange(devices_all, dtype=jnp.int32)[:, None] % N_SK
    owner_dev = peer_index * N_SK + column_index
    return (owner_dev * MRG_DEV + local_id).reshape(-1).astype(jnp.int32)


def draw_text_kv(key, part):
    key = jax.random.fold_in(key, 23)
    key_base, key_gain, key_spread = jax.random.split(key, 3)
    unit_gain = jax.random.uniform(key_gain, (1, 1, HD), jnp.float32, 1.5, 2.5)
    spread = jnp.exp(jax.random.uniform(key_spread, (TEXT, HEADS, 1), jnp.float32, -0.2, 0.2))
    base = jax.random.normal(key_base, (2, TEXT, HEADS, HD), jnp.float32)
    keys = base[0] * unit_gain * spread
    values = base[1]
    return jnp.stack([keys, values]).reshape(2, TEXT, HEADS * HD).astype(jnp.bfloat16)


def levels(key, shape, pieces, smallest, largest):
    factor_of = 1.0
    for dim, blocks in pieces:
        draws = jax.random.uniform(jax.random.fold_in(jax.random.fold_in(key, 6), dim), (blocks,), jnp.float32, smallest / len(pieces), largest / len(pieces))
        factor_of = factor_of * jnp.repeat(jnp.exp(draws), shape[dim] // blocks).reshape((-1,) + (1,) * (len(shape) - 1 - dim))
    return factor_of


def bell_draw(own_key, shape, deviation, limit, cuts=(), kind=jnp.bfloat16):
    drawn = deviation * jax.random.normal(own_key, shape, jnp.float32)
    if cuts:
        drawn = drawn * levels(own_key, shape, cuts, -0.22, 0.18)
    return jnp.clip(drawn, -limit, limit).astype(kind)


def setup_inputs(seed: int = 0) -> dict:
    key_list = jax.random.split(jax.random.key(seed), 7)
    video = bell_draw(key_list[0], (SOURCE, D), 1.0, 6.0, ((0, 256),))
    assign = draw_assign(jax.random.fold_in(key_list[6], 71), 0)
    qkv_weight = bell_draw(key_list[2], (D, HEADS * 3 * HD), D ** -0.5, 0.109375, ((1, 16),))
    qk_gain = jnp.clip(jax.random.uniform(key_list[3], (2, HD), jnp.float32, 1.5, 2.5), 1.5, 2.5)
    text_kv = draw_text_kv(jax.random.fold_in(key_list[6], 71), 0)
    out_weight = bell_draw(key_list[5], (HEADS * HD, D), (HEADS * HD) ** -0.5, 0.125, ((0, 16),))
    return {"video": video, "assign": assign, "qkv_weight": qkv_weight, "qk_gain": qk_gain, "text_kv": text_kv, "out_weight": out_weight}


def rms_norm(values, gain):
    return values * lax.rsqrt(lax.optimization_barrier(jnp.mean(values * values, axis=-1, keepdims=True)) + 1e-06) * gain

def reference(video, assign, qkv_weight, qk_gain, text_kv, out_weight):
    row_totals = jax.ops.segment_sum(video.astype(jnp.float32), assign, num_segments=MERGED)
    counts = jax.ops.segment_sum(jnp.ones(assign.shape, jnp.float32), assign, num_segments=MERGED)
    merged = (row_totals / jnp.maximum(counts, 1.0)[:, None]).astype(jnp.bfloat16)
    head_weights = jnp.transpose(qkv_weight.reshape(D, HEADS, 3, HD), (1, 0, 2, 3))
    text_parts = jnp.transpose(text_kv.reshape(2, TEXT, HEADS, HD), (2, 0, 1, 3))
    score_scale = 1.0 / math.sqrt(HD)

    def one_head(operands):
        weight_head, text_head = operands
        queries = rms_norm(jnp.dot(merged, weight_head[:, 0], preferred_element_type=jnp.float32), qk_gain[0]).astype(jnp.bfloat16)
        own_keys = rms_norm(jnp.dot(merged, weight_head[:, 1], preferred_element_type=jnp.float32), qk_gain[1]).astype(jnp.bfloat16)
        own_values = jnp.dot(merged, weight_head[:, 2], preferred_element_type=jnp.float32).astype(jnp.bfloat16)
        key_rows = jnp.concatenate([own_keys, text_head[0]], axis=0)
        value_rows = jnp.concatenate([own_values, text_head[1]], axis=0)

        def attend(query_block):
            scores = jnp.dot(query_block, key_rows.T, preferred_element_type=jnp.float32) * score_scale
            probs = jnp.exp(scores - lax.optimization_barrier(jnp.max(scores, axis=1, keepdims=True)))
            summed = jnp.dot(probs.astype(jnp.bfloat16), value_rows, preferred_element_type=jnp.float32)
            return (summed / lax.optimization_barrier(jnp.sum(probs, axis=1, keepdims=True))).astype(jnp.bfloat16)
        blocks = queries.reshape(MERGED // (8 * MRG_DEV), 8 * MRG_DEV, HD)
        return lax.map(attend, blocks).reshape(MERGED, HD)
    attended = lax.map(one_head, (head_weights, text_parts))
    attended = jnp.transpose(attended, (1, 0, 2)).reshape(MERGED, HEADS * HD)
    group_width = HEADS_DEV * HD

    def add_group(group, total):
        columns = lax.dynamic_slice_in_dim(attended, group * group_width, group_width, 1)
        weight_rows = lax.dynamic_slice_in_dim(out_weight, group * group_width, group_width, 0)
        partial_out = lax.optimization_barrier(jnp.dot(columns, weight_rows, preferred_element_type=jnp.float32).astype(jnp.bfloat16))
        return total + partial_out.astype(jnp.float32)
    delta = lax.fori_loop(0, N_SQ, add_group, jnp.zeros((MERGED, D), jnp.float32)).astype(jnp.bfloat16)
    return (video.astype(jnp.float32) + delta[assign].astype(jnp.float32)).astype(jnp.bfloat16)
```

```python
import functools
import math

import jax
import jax.numpy as jnp
from jax import lax
from jax.experimental import pallas as pl
from jax.experimental.pallas import tpu as pltpu
from jax.sharding import Mesh, PartitionSpec as P

BF = jnp.bfloat16
F32 = jnp.float32
HD = 128
SQ = 16
SK = 16
CAP = 24
MRG = 48
SRC = 192
ROWS = SQ * MRG
TEXT = 256
D = 3072


def dot(a, b):
    return lax.dot_general(a, b, (((1,), (0,)), ((), ())), preferred_element_type=F32)


def dot_t(a, b):
    return lax.dot_general(a, b, (((1,), (1,)), ((), ())), preferred_element_type=F32)


def pack_kernel(row_ref, col_ref, video_ref, out_ref):
    peer_row = row_ref[...] // (MRG * SK)
    peer_col = col_ref[...] // (MRG * SK)
    before = lax.broadcasted_iota(jnp.int32, (SRC, SRC), 0) < lax.broadcasted_iota(
        jnp.int32, (SRC, SRC), 1
    )
    same = jnp.where(before & (peer_row == peer_col), 1.0, 0.0)
    rank = jnp.sum(same, axis=0, keepdims=True).astype(jnp.int32)
    position = peer_row * CAP + rank
    slots = lax.broadcasted_iota(jnp.int32, (SQ * CAP, SRC), 0)
    hot = jnp.where(slots == position, 1.0, 0.0).astype(BF)
    out_ref[...] = dot(hot, video_ref[...]).astype(BF)


def pack_rows(assign, video):
    width = 768
    return pl.pallas_call(
        pack_kernel,
        grid=(D // width,),
        in_specs=[
            pl.BlockSpec((1, SRC), lambda c: (0, 0)),
            pl.BlockSpec((SRC, 1), lambda c: (0, 0)),
            pl.BlockSpec((SRC, width), lambda c: (0, c)),
        ],
        out_specs=pl.BlockSpec((SQ * CAP, width), lambda c: (0, c)),
        out_shape=jax.ShapeDtypeStruct((SQ * CAP, D), BF),
        compiler_params=pltpu.CompilerParams(vmem_limit_bytes=32 << 20),
        name="pack_rows",
    )(assign.reshape(1, SRC), assign.reshape(SRC, 1), video)


def project_kernel(rows_ref, weight_ref, gain_ref, q_ref, kv_ref):
    full = dot(rows_ref[...], weight_ref[...])

    def norm(part, gain):
        return part * lax.rsqrt(jnp.mean(part * part, axis=-1, keepdims=True) + 1e-06) * gain

    factor = math.log2(math.e) / math.sqrt(HD)
    q_ref[...] = (norm(full[:, :HD], gain_ref[0:1, :]) * factor).astype(BF)
    kv_ref[:, :HD] = norm(full[:, HD : 2 * HD], gain_ref[1:2, :]).astype(BF)
    kv_ref[:, HD:] = full[:, 2 * HD :].astype(BF)


def project(rows, weight, gain):
    count = rows.shape[0]
    step = 128
    return pl.pallas_call(
        project_kernel,
        grid=(count // step,),
        in_specs=[
            pl.BlockSpec((step, D), lambda r: (r, 0)),
            pl.BlockSpec((D, 3 * HD), lambda r: (0, 0)),
            pl.BlockSpec((2, HD), lambda r: (0, 0)),
        ],
        out_specs=[
            pl.BlockSpec((step, HD), lambda r: (r, 0)),
            pl.BlockSpec((step, 2 * HD), lambda r: (r, 0)),
        ],
        out_shape=[
            jax.ShapeDtypeStruct((count, HD), BF),
            jax.ShapeDtypeStruct((count, 2 * HD), BF),
        ],
        compiler_params=pltpu.CompilerParams(vmem_limit_bytes=32 << 20),
        name="project",
    )(rows, weight, gain)


QB = 256


def absorb(q_ref, m_ref, l_ref, acc_ref, keys, values, first):
    for block in range(ROWS // QB):
        span = pl.ds(block * QB, QB)
        scores = dot_t(q_ref[span, :], keys)
        top = jnp.max(scores, axis=-1, keepdims=True)
        if first:
            raised = top
        else:
            before = m_ref[span, :1]
            raised = jnp.maximum(before, top)
            fading = jnp.exp2(before - raised)
        probs = jnp.exp2(scores - raised)
        total = jnp.sum(probs, axis=-1, keepdims=True)
        update = dot(probs.astype(BF), values)
        if first:
            l_ref[span, :] = jnp.broadcast_to(total, (QB, HD))
            acc_ref[span, :] = update
        else:
            l_ref[span, :] = l_ref[span, :] * fading + total
            acc_ref[span, :] = acc_ref[span, :] * fading + update
        m_ref[span, :] = jnp.broadcast_to(raised, (QB, HD))


def attend_kernel(need_ref, q_ref, text_ref, kv_ref, out_ref, m_ref, l_ref, acc_ref, done_ref):
    step = pl.program_id(0)

    @pl.when(step == 0)
    def _():
        absorb(q_ref, m_ref, l_ref, acc_ref, text_ref[0], text_ref[1], True)

    chunk = 768

    for part in range(kv_ref.shape[0] // chunk):
        span = pl.ds(part * chunk, chunk)
        absorb(q_ref, m_ref, l_ref, acc_ref, kv_ref[span, :HD], kv_ref[span, HD:], False)

    @pl.when(step == pl.num_programs(0) - 1)
    def _():
        done_ref[...] = (acc_ref[...] / l_ref[...]).astype(BF)
        attended = done_ref[...]
        for peer in range(SQ):
            hot = jnp.where(
                lax.broadcasted_iota(jnp.int32, (SRC, ROWS), 1) == need_ref[peer], 1.0, 0.0
            ).astype(BF)
            out_ref[peer] = dot(hot, attended).astype(BF)


def attend(need, queries, text, kv):
    step = 1536
    return pl.pallas_call(
        attend_kernel,
        grid=(kv.shape[0] // step,),
        in_specs=[
            pl.BlockSpec((SQ, SRC, 1), lambda k: (0, 0, 0)),
            pl.BlockSpec((ROWS, HD), lambda k: (0, 0)),
            pl.BlockSpec((2, TEXT, HD), lambda k: (0, 0, 0)),
            pl.BlockSpec((step, 2 * HD), lambda k: (k, 0)),
        ],
        out_specs=pl.BlockSpec((SQ, SRC, HD), lambda k: (0, 0, 0)),
        out_shape=jax.ShapeDtypeStruct((SQ, SRC, HD), BF),
        scratch_shapes=[
            pltpu.VMEM((ROWS, HD), F32),
            pltpu.VMEM((ROWS, HD), F32),
            pltpu.VMEM((ROWS, HD), F32),
            pltpu.VMEM((ROWS, HD), BF),
        ],
        compiler_params=pltpu.CompilerParams(vmem_limit_bytes=48 << 20),
        name="attend",
    )(need, queries, text, kv)


def finish_kernel(core_ref, parts_ref, own_ref, other_ref, video_ref, out_ref, flat_ref):
    step = pl.program_id(0)
    half = pl.num_programs(0) // 2

    @pl.when(step == 0)
    def _():
        for group in range(SQ):
            flat_ref[:, group * HD : (group + 1) * HD] = parts_ref[group]

    def product(weight_ref):
        delta = dot(flat_ref[...], weight_ref[...]).astype(BF).astype(F32)
        out_ref[...] = (video_ref[...].astype(F32) + delta).astype(BF)

    @pl.when(step < half)
    def _():
        product(own_ref)

    @pl.when(step >= half)
    def _():
        product(other_ref)


def finish(core, parts, own, other, video):
    width = 512
    half = D // 2 // width

    def place(step, core_ref):
        return (0, lax.rem(step + half * core_ref[0], 2 * half))

    return pl.pallas_call(
        finish_kernel,
        grid_spec=pltpu.PrefetchScalarGridSpec(
            num_scalar_prefetch=1,
            grid=(2 * half,),
            in_specs=[
                pl.BlockSpec((SQ, SRC, HD), lambda c, core_ref: (0, 0, 0)),
                pl.BlockSpec((SQ * HD, width), lambda c, core_ref: (0, jnp.minimum(c, half - 1))),
                pl.BlockSpec((SQ * HD, width), lambda c, core_ref: (0, jnp.maximum(c - half, 0))),
                pl.BlockSpec((SRC, width), place),
            ],
            out_specs=pl.BlockSpec((SRC, width), place),
            scratch_shapes=[pltpu.VMEM((SRC, SQ * HD), BF)],
        ),
        out_shape=jax.ShapeDtypeStruct((SRC, D), BF),
        compiler_params=pltpu.CompilerParams(vmem_limit_bytes=32 << 20),
        name="finish",
    )(core, parts, own, other, video)


def member_of(all_assign, mine):
    peers = all_assign // (MRG * SK)
    local = (all_assign % MRG).astype(F32)
    chosen = (peers == mine).astype(F32)
    triangle = jnp.triu(jnp.ones((SRC, SRC), F32), 1)
    rank = dot(chosen.astype(BF), triangle.astype(BF))
    slots = jnp.arange(CAP, dtype=F32)
    placed = jnp.where(rank[:, None, :] == slots[None, :, None], chosen[:, None, :], 0.0)
    ids = jnp.sum(placed * (local + 1.0)[:, None, :], axis=2) - 1.0
    flat = ids.reshape(SQ * CAP)
    return (jnp.arange(MRG, dtype=F32)[:, None] == flat[None, :]).astype(BF)


def per_device(video, assign, qkv_weight, qk_gain, text_kv, out_weight):
    mine = lax.axis_index(("x", "y"))
    core = lax.axis_index("c")
    all_assign = lax.all_gather(assign.reshape(1, SRC), ("x", "y"), axis=0, tiled=True)
    half_weight = lax.dynamic_slice_in_dim(out_weight, core * (D // 2), D // 2, 1)
    own_half = lax.all_gather(half_weight, ("x", "y"), axis=0, tiled=True)

    send = pack_rows(assign, video).reshape(SQ, CAP, D)
    got = lax.all_to_all(send, ("x", "y"), split_axis=0, concat_axis=0, tiled=True)
    member = member_of(all_assign, mine)
    need = (all_assign // (MRG * SK)) * MRG + all_assign % MRG
    counts = jnp.sum(member.astype(F32), axis=1)
    totals = dot(member, got.reshape(SQ * CAP, D))
    merged = (totals / jnp.maximum(counts, 1.0)[:, None]).astype(BF)

    merged, own_half = lax.optimization_barrier((merged, own_half))
    rows = lax.all_gather(merged, ("x", "y"), axis=0, tiled=True)
    other_half = lax.ppermute(own_half, "c", [(0, 1), (1, 0)])
    queries, kv = project(rows, qkv_weight, qk_gain)
    all_kv = lax.all_gather(kv, ("z", "c"), axis=0, tiled=True)
    parts = attend(need.reshape(SQ, SRC, 1), queries, text_kv, all_kv)
    parts = lax.all_to_all(parts, ("x", "y"), split_axis=0, concat_axis=0, tiled=True)
    return finish(core.astype(jnp.int32).reshape(1), parts, own_half, other_half, video)


def solution(mesh):
    fine = Mesh(mesh.devices.reshape(4, 4, 8, 2), ("x", "y", "z", "c"))
    sq = ("x", "y")
    in_specs = (
        P(("x", "y", "z", "c"), None),
        P(("x", "y", "z", "c")),
        P(None, sq),
        P(),
        P(None, None, sq),
        P(sq, None),
    )
    out_specs = P(("x", "y", "z", "c"), None)
    return jax.shard_map(
        per_device, mesh=fine, in_specs=in_specs, out_specs=out_specs, check_vma=False
    )
```

```python
import functools
import math

import jax
import jax.numpy as jnp
from jax import lax
from jax.experimental import pallas as pl
from jax.experimental.pallas import tpu as pltpu
from jax.sharding import Mesh, PartitionSpec as P

BF = jnp.bfloat16
F32 = jnp.float32
HD = 128
SQ = 16
SK = 16
CAP = 24
MRG = 48
SRC = 192
ROWS = SQ * MRG
TEXT = 256
D = 3072


def dot(a, b):
    return lax.dot_general(a, b, (((1,), (0,)), ((), ())), preferred_element_type=F32)


def dot_t(a, b):
    return lax.dot_general(a, b, (((1,), (1,)), ((), ())), preferred_element_type=F32)


def pack_kernel(row_ref, col_ref, video_ref, out_ref):
    peer_row = row_ref[...] // (MRG * SK)
    peer_col = col_ref[...] // (MRG * SK)
    before = lax.broadcasted_iota(jnp.int32, (SRC, SRC), 0) < lax.broadcasted_iota(
        jnp.int32, (SRC, SRC), 1
    )
    same = jnp.where(before & (peer_row == peer_col), 1.0, 0.0)
    rank = jnp.sum(same, axis=0, keepdims=True).astype(jnp.int32)
    position = peer_row * CAP + rank
    slots = lax.broadcasted_iota(jnp.int32, (SQ * CAP, SRC), 0)
    hot = jnp.where(slots == position, 1.0, 0.0).astype(BF)
    out_ref[...] = dot(hot, video_ref[...]).astype(BF)


def pack_rows(assign, video):
    width = 768
    return pl.pallas_call(
        pack_kernel,
        grid=(D // width,),
        in_specs=[
            pl.BlockSpec((1, SRC), lambda c: (0, 0)),
            pl.BlockSpec((SRC, 1), lambda c: (0, 0)),
            pl.BlockSpec((SRC, width), lambda c: (0, c)),
        ],
        out_specs=pl.BlockSpec((SQ * CAP, width), lambda c: (0, c)),
        out_shape=jax.ShapeDtypeStruct((SQ * CAP, D), BF),
        compiler_params=pltpu.CompilerParams(vmem_limit_bytes=32 << 20),
        name="pack_rows",
    )(assign.reshape(1, SRC), assign.reshape(SRC, 1), video)


def project_kernel(*refs):
    *row_refs, weight_ref, gain_ref, q_ref, kv_ref = refs

    def norm(part, gain):
        return part * lax.rsqrt(jnp.mean(part * part, axis=-1, keepdims=True) + 1e-06) * gain

    factor = math.log2(math.e) / math.sqrt(HD)
    start = 0
    for row_ref in row_refs:
        span = pl.ds(start, row_ref.shape[0])
        start += row_ref.shape[0]
        full = dot(row_ref[...], weight_ref[...])
        q_ref[span, :] = (norm(full[:, :HD], gain_ref[0:1, :]) * factor).astype(BF)
        kv_ref[span, :HD] = norm(full[:, HD : 2 * HD], gain_ref[1:2, :]).astype(BF)
        kv_ref[span, HD:] = full[:, 2 * HD :].astype(BF)


def project(pieces, weight, gain):
    count = sum(piece.shape[0] for piece in pieces)
    return pl.pallas_call(
        project_kernel,
        out_shape=[
            jax.ShapeDtypeStruct((count, HD), BF),
            jax.ShapeDtypeStruct((count, 2 * HD), BF),
        ],
        compiler_params=pltpu.CompilerParams(vmem_limit_bytes=32 << 20),
        cost_estimate=pl.CostEstimate(
            flops=2 * count * D * 3 * HD, bytes_accessed=2 * D * (count + 3 * HD), transcendentals=0
        ),
        name="project",
    )(*pieces, weight, gain)


QB = 256
CHUNK = 768


def attend_kernel(first, last, pieces, *refs):
    q_ref, *refs = refs
    text_ref = refs.pop(0) if first else None
    kv_refs = [refs.pop(0) for _ in range(pieces)]
    if not first:
        m_in, acc_in = refs.pop(0), refs.pop(0)
    if last:
        need_ref, ids_ref, out_ref, m_ref, acc_ref, wide_ref, done_ref = refs
    else:
        m_ref, acc_ref, wide_ref = refs

    wide_ref[:, HD:] = jnp.ones((wide_ref.shape[0], HD), BF)
    chunks = []
    place = 0
    if first:
        wide_ref[:TEXT, :HD] = text_ref[1]
        chunks.append((text_ref[0], 0, TEXT))
        place = TEXT
    for ref in kv_refs:
        size = ref.shape[0]
        wide_ref[place : place + size, :HD] = ref[:, HD:]
        for start in range(0, size, CHUNK):
            width = min(CHUNK, size - start)
            chunks.append((ref[start : start + width, :HD], place + start, width))
        place += size

    for index, (keys, start, width) in enumerate(chunks):
        values = wide_ref[start : start + width, :]
        fresh = first and index == 0
        from_m, from_acc = (m_in, acc_in) if index == 0 and not first else (m_ref, acc_ref)
        for block in range(ROWS // QB):
            span = pl.ds(block * QB, QB)
            scores = dot_t(q_ref[span, :], keys)
            raised = jnp.max(scores, axis=-1, keepdims=True)
            if not fresh:
                before = from_m[span, :1]
                raised = jnp.maximum(before, raised)
                fading = jnp.exp2(before - raised)
            probs = jnp.exp2(scores - raised).astype(BF)
            update = dot(probs, values)
            if not fresh:
                update = from_acc[span, :] * fading + update
            acc_ref[span, :] = update
            m_ref[span, :] = jnp.broadcast_to(raised, (QB, HD))

    if last:
        done_ref[...] = (acc_ref[:, :HD] / acc_ref[:, HD:]).astype(BF)
        for peer in range(SQ):
            need = need_ref[peer * SRC : (peer + 1) * SRC, :]
            wanted = need[:, :1].astype(F32) * MRG + need[:, 1:2].astype(F32)
            hot = jnp.where(wanted == ids_ref[...], 1.0, 0.0).astype(BF)
            out_ref[peer] = dot(hot, done_ref[...]).astype(BF)


def attend(queries, kv, state=None, text=None, finish_with=None):
    first, last = text is not None, finish_with is not None
    keys = sum(piece.shape[0] for piece in kv) + (TEXT if first else 0)
    shapes = [(ROWS, HD), (ROWS, 2 * HD)]
    scratch = [pltpu.VMEM((keys, 2 * HD), BF)]
    operands = [queries] + ([text] if first else []) + list(kv) + ([] if first else list(state))
    if last:
        operands += list(finish_with)
        out_shape = jax.ShapeDtypeStruct((SQ, SRC, HD), BF)
        scratch = [pltpu.VMEM(shape, F32) for shape in shapes] + scratch
        scratch.append(pltpu.VMEM((ROWS, HD), BF))
    else:
        out_shape = [jax.ShapeDtypeStruct(shape, F32) for shape in shapes]
    return pl.pallas_call(
        functools.partial(attend_kernel, first, last, len(kv)),
        out_shape=out_shape,
        scratch_shapes=scratch,
        compiler_params=pltpu.CompilerParams(vmem_limit_bytes=40 << 20),
        cost_estimate=pl.CostEstimate(
            flops=6 * ROWS * keys * HD,
            bytes_accessed=4 * keys * HD,
            transcendentals=ROWS * keys,
        ),
        name="attend",
    )(*operands)


def finish_kernel(core_ref, parts_ref, *refs):
    *weight_refs, video_ref, mark_ref, out_ref, flat_ref = refs
    step = pl.program_id(0)

    @pl.when(step == 0)
    def _():
        for group in range(SQ):
            flat_ref[:, group * HD : (group + 1) * HD] = parts_ref[group]

    for index, weight_ref in enumerate(weight_refs):

        @pl.when(step == index)
        def _():
            delta = dot(flat_ref[...], weight_ref[...]).astype(BF).astype(F32)
            out_ref[...] = (video_ref[...].astype(F32) + delta).astype(BF)


def finish(core, parts, weights, video, mark):
    count = len(weights)
    width = D // count

    def place(step, core_ref):
        return (0, lax.rem(step + count // 2 * core_ref[0], count))

    return pl.pallas_call(
        finish_kernel,
        grid_spec=pltpu.PrefetchScalarGridSpec(
            num_scalar_prefetch=1,
            grid=(count,),
            in_specs=[pl.BlockSpec((SQ, SRC, HD), lambda c, core_ref: (0, 0, 0))]
            + [pl.BlockSpec((SQ * HD, width), lambda c, core_ref: (0, 0))] * count
            + [pl.BlockSpec((SRC, width), place)]
            + [pl.BlockSpec((16, HD), lambda c, core_ref: (0, 0))],
            out_specs=pl.BlockSpec((SRC, width), place),
            scratch_shapes=[pltpu.VMEM((SRC, SQ * HD), BF)],
        ),
        out_shape=jax.ShapeDtypeStruct((SRC, D), BF),
        compiler_params=pltpu.CompilerParams(vmem_limit_bytes=40 << 20),
        name="finish",
    )(core, parts, *weights, video, mark)


def member_of(peers, local, mine):
    chosen = (peers == mine).astype(F32)
    triangle = jnp.triu(jnp.ones((SRC, SRC), F32), 1)
    rank = dot(chosen.astype(BF), triangle.astype(BF))
    slots = jnp.arange(CAP, dtype=F32)
    placed = jnp.where(rank[:, None, :] == slots[None, :, None], chosen[:, None, :], 0.0)
    ids = jnp.sum(placed * (local + 1.0)[:, None, :], axis=2) - 1.0
    flat = ids.reshape(SQ * CAP)
    return (jnp.arange(MRG, dtype=F32)[:, None] == flat[None, :]).astype(BF)


SIZE = {"x": 4, "y": 4, "z": 8, "c": 2}


def shift(value, axis, by):
    size = SIZE[axis]
    return lax.ppermute(value, axis, [(i, (i + by) % size) for i in range(size)])


def cat(*pieces):
    return jnp.concatenate(pieces, axis=0)


def gather_rows(merged):
    half = MRG // 2
    a, b = merged[:half], merged[half:]
    a_near = [shift(a, "x", k) for k in (1, -1, 2)]
    b_near = [shift(b, "y", k) for k in (1, -1, 2)]
    a_line, b_line = cat(a, *a_near), cat(b, *b_near)
    a_up, a_down = shift(a_line, "y", 1), shift(a_line, "y", -1)
    b_up, b_down = shift(b_line, "x", 1), shift(b_line, "x", -1)
    cut = MRG
    far = [
        shift(a_up[:cut], "y", 1),
        shift(a_down[cut:], "y", -1),
        shift(b_up[:cut], "x", 1),
        shift(b_down[cut:], "x", -1),
    ]
    return [a_line, b_line], [a_up, a_down, b_up, b_down], far


def row_ids():
    x, y = lax.axis_index("x"), lax.axis_index("y")
    near = (0, -1, 1, 2)
    places = [(k, 0, 0) for k in near] + [(0, k, 1) for k in near]
    places += [(k, -1, 0) for k in near] + [(k, 1, 0) for k in near]
    places += [(-1, k, 1) for k in near] + [(1, k, 1) for k in near]
    places += [(k, 2, 0) for k in near] + [(2, k, 1) for k in near]
    dx, dy, part = (jnp.array(column, jnp.int32) for column in zip(*places))
    owner = (x + dx) % 4 * 4 + (y + dy) % 4
    half = MRG // 2
    ids = (owner * MRG + part * half)[:, None] + jnp.arange(half, dtype=jnp.int32)[None, :]
    return ids.reshape(1, ROWS).astype(F32)


def per_device(video, assign, qkv_weight, qk_gain, text_kv, out_weight):
    sq = ("x", "y")
    mine = lax.axis_index(sq).astype(F32)
    core = lax.axis_index("c")
    peer = (assign // (MRG * SK)).astype(F32)
    local = (assign % MRG).astype(F32)
    lane = jnp.arange(HD)[None, :]
    tags = jnp.where(lane == 0, peer[:, None], jnp.where(lane == 1, local[:, None], 0.0)).astype(BF)
    all_tags = lax.all_gather(tags, sq, axis=0, tiled=True)

    send = pack_rows(assign, video).reshape(SQ, CAP, D)
    got = lax.all_to_all(send, sq, split_axis=0, concat_axis=0, tiled=True)
    peers = all_tags[:, 0].astype(F32).reshape(SQ, SRC)
    locals_ = all_tags[:, 1].astype(F32).reshape(SQ, SRC)
    member = member_of(peers, locals_, mine)
    counts = jnp.sum(member.astype(F32), axis=1)
    totals = dot(member, got.reshape(SQ * CAP, D))
    merged = (totals / jnp.maximum(counts, 1.0)[:, None]).astype(BF)

    sets = gather_rows(merged)
    projected = [project(rows, qkv_weight, qk_gain) for rows in sets]
    queries = cat(*[q for q, _ in projected])
    kv = cat(*[kv for _, kv in projected])

    half_weight = lax.dynamic_slice_in_dim(out_weight, core * (D // 2), D // 2, 1)
    half_weight, kv = lax.optimization_barrier((half_weight, kv))
    own = [
        lax.all_gather(part, sq, axis=0, tiled=True) for part in jnp.split(half_weight, 2, axis=1)
    ]
    state = attend(queries, [kv], text=text_kv)
    swapped = [shift(kv, "c", 1)]
    up = down = kv
    for _ in range(3):
        up, down = shift(up, "z", 1), shift(down, "z", -1)
        state, up, down = lax.optimization_barrier((state, up, down))
        state = attend(queries, [up, down] + swapped, state)
        swapped = [shift(up, "c", 1), shift(down, "c", 1)]
    cut = ROWS // 2
    up, down = shift(up[:cut], "z", 1), shift(down[cut:], "z", -1)
    state, up, down = lax.optimization_barrier((state, up, down))
    state = attend(queries, [up, down] + swapped, state)
    swapped = [shift(up, "c", 1), shift(down, "c", 1)]
    own[0], state = lax.optimization_barrier((own[0], state))
    parts = attend(queries, swapped, state, finish_with=(all_tags, row_ids()))
    other = [shift(own[0], "c", 1)]
    parts = lax.all_to_all(parts, sq, split_axis=0, concat_axis=0, tiled=True)
    own[1], mark = lax.optimization_barrier((own[1], parts[0, :16]))
    other.append(shift(own[1], "c", 1))
    return finish(core.astype(jnp.int32).reshape(1), parts, own + other, video, mark)


def solution(mesh):
    fine = Mesh(mesh.devices.reshape(4, 4, 8, 2), ("x", "y", "z", "c"))
    sq = ("x", "y")
    in_specs = (
        P(("x", "y", "z", "c"), None),
        P(("x", "y", "z", "c")),
        P(None, sq),
        P(),
        P(None, None, sq),
        P(sq, None),
    )
    out_specs = P(("x", "y", "z", "c"), None)
    return jax.shard_map(
        per_device, mesh=fine, in_specs=in_specs, out_specs=out_specs, check_vma=False
    )
```

```python
import functools
import math

import jax
import jax.numpy as jnp
from jax import lax
from jax.experimental import pallas as pl
from jax.experimental.pallas import tpu as pltpu
from jax.sharding import Mesh, PartitionSpec as P

BF = jnp.bfloat16
F32 = jnp.float32
HD = 128
SQ = 16
SK = 16
CAP = 24
MRG = 48
SRC = 192
ROWS = SQ * MRG
TEXT = 256
D = 3072


def dot(a, b):
    return lax.dot_general(a, b, (((1,), (0,)), ((), ())), preferred_element_type=F32)


def dot_t(a, b):
    return lax.dot_general(a, b, (((1,), (1,)), ((), ())), preferred_element_type=F32)


WIDE = D + HD
HALF = SRC // 2


def pack_kernel(row_ref, col_ref, pair_ref, video_ref, out_ref, tags_ref):
    peer_row = row_ref[...] // (MRG * SK)
    peer_col = col_ref[...] // (MRG * SK)
    before = lax.broadcasted_iota(jnp.int32, (SRC, SRC), 0) < lax.broadcasted_iota(
        jnp.int32, (SRC, SRC), 1
    )
    same = jnp.where(before & (peer_row == peer_col), 1.0, 0.0)
    rank = jnp.sum(same, axis=0, keepdims=True).astype(jnp.int32)
    position = peer_row * CAP + rank
    slots = lax.broadcasted_iota(jnp.int32, (SQ * CAP, SRC), 0)
    chosen = slots == position
    out_ref[:, :D] = dot(jnp.where(chosen, 1.0, 0.0).astype(BF), video_ref[...]).astype(BF)
    number = (row_ref[...] % MRG + 1).astype(F32)
    slot_number = jnp.sum(jnp.where(chosen, number, 0.0), axis=1, keepdims=True)
    lanes = lax.broadcasted_iota(jnp.int32, (SQ * CAP, HD), 1)
    tags_ref[...] = jnp.where(lanes == HD - 1, slot_number, 0.0)
    pair = pair_ref[...]
    for peer in range(SQ):
        tags_ref[peer * CAP : peer * CAP + 2, :HALF] = (pair // (MRG * SK)).astype(F32)
        tags_ref[peer * CAP + 2 : peer * CAP + 4, :HALF] = (pair % MRG).astype(F32)
    out_ref[:, D:] = tags_ref[...].astype(BF)


def pack_rows(assign, video):
    return pl.pallas_call(
        pack_kernel,
        out_shape=jax.ShapeDtypeStruct((SQ * CAP, WIDE), BF),
        scratch_shapes=[pltpu.VMEM((SQ * CAP, HD), F32)],
        compiler_params=pltpu.CompilerParams(vmem_limit_bytes=32 << 20),
        name="pack_rows",
    )(assign.reshape(1, SRC), assign.reshape(SRC, 1), assign.reshape(2, HALF), video)


def merge_kernel(got_ref, out_ref):
    number = got_ref[:, WIDE - 1 :].astype(F32)
    places = lax.broadcasted_iota(jnp.int32, (SQ * CAP, MRG), 1).astype(F32) + 1.0
    member = jnp.where(number == places, 1.0, 0.0).astype(BF)

    def over_slots(values):
        return lax.dot_general(
            member, values, (((0,), (0,)), ((), ())), preferred_element_type=F32
        )

    counts = over_slots(jnp.ones((SQ * CAP, HD), BF))[:, :1]
    out_ref[...] = (over_slots(got_ref[:, :D]) / jnp.maximum(counts, 1.0)).astype(BF)


def merge_rows(got):
    return pl.pallas_call(
        merge_kernel,
        out_shape=jax.ShapeDtypeStruct((MRG, D), BF),
        compiler_params=pltpu.CompilerParams(vmem_limit_bytes=32 << 20),
        name="merge_rows",
    )(got)


def project_kernel(*refs):
    *row_refs, weight_ref, gain_ref, q_ref, kv_ref = refs

    def norm(part, gain):
        return part * lax.rsqrt(jnp.mean(part * part, axis=-1, keepdims=True) + 1e-06) * gain

    factor = math.log2(math.e) / math.sqrt(HD)
    start = 0
    for row_ref in row_refs:
        span = pl.ds(start, row_ref.shape[0])
        start += row_ref.shape[0]
        full = dot(row_ref[...], weight_ref[...])
        q_ref[span, :] = (norm(full[:, :HD], gain_ref[0:1, :]) * factor).astype(BF)
        kv_ref[span, :HD] = norm(full[:, HD : 2 * HD], gain_ref[1:2, :]).astype(BF)
        kv_ref[span, HD:] = full[:, 2 * HD :].astype(BF)


def project(pieces, weight, gain):
    count = sum(piece.shape[0] for piece in pieces)
    return pl.pallas_call(
        project_kernel,
        out_shape=[
            jax.ShapeDtypeStruct((count, HD), BF),
            jax.ShapeDtypeStruct((count, 2 * HD), BF),
        ],
        compiler_params=pltpu.CompilerParams(vmem_limit_bytes=32 << 20),
        cost_estimate=pl.CostEstimate(
            flops=2 * count * D * 3 * HD, bytes_accessed=2 * D * (count + 3 * HD), transcendentals=0
        ),
        name="project",
    )(*pieces, weight, gain)


QB = 256
CHUNK = 768


def attend_kernel(first, last, pieces, *refs):
    q_ref, *refs = refs
    text_ref = refs.pop(0) if first else None
    kv_refs = [refs.pop(0) for _ in range(pieces)]
    if not first:
        m_in, acc_in = refs.pop(0), refs.pop(0)
    if last:
        need_ref, ids_ref, out_ref, m_ref, acc_ref, wide_ref, done_ref = refs
    else:
        m_ref, acc_ref, wide_ref = refs

    wide_ref[:, HD:] = jnp.ones((wide_ref.shape[0], HD), BF)
    chunks = []
    place = 0
    if first:
        wide_ref[:TEXT, :HD] = text_ref[1]
        chunks.append((text_ref[0], 0, TEXT))
        place = TEXT
    for ref in kv_refs:
        size = ref.shape[0]
        wide_ref[place : place + size, :HD] = ref[:, HD:]
        for start in range(0, size, CHUNK):
            width = min(CHUNK, size - start)
            chunks.append((ref[start : start + width, :HD], place + start, width))
        place += size

    for index, (keys, start, width) in enumerate(chunks):
        values = wide_ref[start : start + width, :]
        fresh = first and index == 0
        from_m, from_acc = (m_in, acc_in) if index == 0 and not first else (m_ref, acc_ref)
        for block in range(ROWS // QB):
            span = pl.ds(block * QB, QB)
            scores = dot_t(q_ref[span, :], keys)
            raised = jnp.max(scores, axis=-1, keepdims=True)
            if not fresh:
                before = from_m[span, :1]
                raised = jnp.maximum(before, raised)
                fading = jnp.exp2(before - raised)
            probs = jnp.exp2(scores - raised).astype(BF)
            update = dot(probs, values)
            if not fresh:
                update = from_acc[span, :] * fading + update
            acc_ref[span, :] = update
            m_ref[span, :] = jnp.broadcast_to(raised, (QB, HD))

    if last:
        done_ref[...] = (acc_ref[:, :HD] / acc_ref[:, HD:]).astype(BF)
        for peer in range(SQ):
            wanted = need_ref[:, peer : peer + 1]
            hot = jnp.where(wanted == ids_ref[...], 1.0, 0.0).astype(BF)
            out_ref[peer] = dot(hot, done_ref[...]).astype(BF)


def attend(queries, kv, state=None, text=None, finish_with=None):
    first, last = text is not None, finish_with is not None
    keys = sum(piece.shape[0] for piece in kv) + (TEXT if first else 0)
    shapes = [(ROWS, HD), (ROWS, 2 * HD)]
    scratch = [pltpu.VMEM((keys, 2 * HD), BF)]
    operands = [queries] + ([text] if first else []) + list(kv) + ([] if first else list(state))
    if last:
        operands += list(finish_with)
        out_shape = jax.ShapeDtypeStruct((SQ, SRC, HD), BF)
        scratch = [pltpu.VMEM(shape, F32) for shape in shapes] + scratch
        scratch.append(pltpu.VMEM((ROWS, HD), BF))
    else:
        out_shape = [jax.ShapeDtypeStruct(shape, F32) for shape in shapes]
    return pl.pallas_call(
        functools.partial(attend_kernel, first, last, len(kv)),
        out_shape=out_shape,
        scratch_shapes=scratch,
        compiler_params=pltpu.CompilerParams(vmem_limit_bytes=40 << 20),
        cost_estimate=pl.CostEstimate(
            flops=6 * ROWS * keys * HD,
            bytes_accessed=4 * keys * HD,
            transcendentals=ROWS * keys,
        ),
        name="attend",
    )(*operands)


def finish_kernel(core_ref, parts_ref, own_ref, other_ref, video_ref, mark_ref, out_ref, flat_ref):
    step = pl.program_id(0)
    half = pl.num_programs(0) // 2

    @pl.when(step == 0)
    def _():
        for group in range(SQ):
            flat_ref[:, group * HD : (group + 1) * HD] = parts_ref[group]

    def product(weight_ref):
        delta = dot(flat_ref[...], weight_ref[...]).astype(BF).astype(F32)
        out_ref[...] = (video_ref[...].astype(F32) + delta).astype(BF)

    @pl.when(step < half)
    def _():
        product(own_ref)

    @pl.when(step >= half)
    def _():
        product(other_ref)


def finish(core, parts, own, other, video, mark):
    width = 512
    half = D // 2 // width

    def place(step, core_ref):
        return (0, lax.rem(step + half * core_ref[0], 2 * half))

    return pl.pallas_call(
        finish_kernel,
        grid_spec=pltpu.PrefetchScalarGridSpec(
            num_scalar_prefetch=1,
            grid=(2 * half,),
            in_specs=[
                pl.BlockSpec((SQ, SRC, HD), lambda c, core_ref: (0, 0, 0)),
                pl.BlockSpec((SQ * HD, width), lambda c, core_ref: (0, jnp.minimum(c, half - 1))),
                pl.BlockSpec((SQ * HD, width), lambda c, core_ref: (0, jnp.maximum(c - half, 0))),
                pl.BlockSpec((SRC, width), place),
                pl.BlockSpec((16, HD), lambda c, core_ref: (0, 0)),
            ],
            out_specs=pl.BlockSpec((SRC, width), place),
            scratch_shapes=[pltpu.VMEM((SRC, SQ * HD), BF)],
        ),
        out_shape=jax.ShapeDtypeStruct((SRC, D), BF),
        compiler_params=pltpu.CompilerParams(vmem_limit_bytes=32 << 20),
        name="finish",
    )(core, parts, own, other, video, mark)


SIZE = {"x": 4, "y": 4, "z": 8, "c": 2}


def shift(value, axis, by):
    size = SIZE[axis]
    return lax.ppermute(value, axis, [(i, (i + by) % size) for i in range(size)])


def cat(*pieces):
    return jnp.concatenate(pieces, axis=0)


def gather_rows(merged):
    half = MRG // 2
    a, b = merged[:half], merged[half:]
    a_near = [shift(a, "x", k) for k in (1, -1, 2)]
    b_near = [shift(b, "y", k) for k in (1, -1, 2)]
    a_line, b_line = cat(a, *a_near), cat(b, *b_near)
    a_up, a_down = shift(a_line, "y", 1), shift(a_line, "y", -1)
    b_up, b_down = shift(b_line, "x", 1), shift(b_line, "x", -1)
    cut = MRG
    far = [
        shift(a_up[:cut], "y", 1),
        shift(a_down[cut:], "y", -1),
        shift(b_up[:cut], "x", 1),
        shift(b_down[cut:], "x", -1),
    ]
    return [a_line, b_line], [a_up, a_down, b_up, b_down], far


def row_ids():
    x, y = lax.axis_index("x"), lax.axis_index("y")
    near = (0, -1, 1, 2)
    places = [(k, 0, 0) for k in near] + [(0, k, 1) for k in near]
    places += [(k, -1, 0) for k in near] + [(k, 1, 0) for k in near]
    places += [(-1, k, 1) for k in near] + [(1, k, 1) for k in near]
    places += [(k, 2, 0) for k in near] + [(2, k, 1) for k in near]
    dx, dy, part = (jnp.array(column, jnp.int32) for column in zip(*places))
    owner = (x + dx) % 4 * 4 + (y + dy) % 4
    half = MRG // 2
    ids = (owner * MRG + part * half)[:, None] + jnp.arange(half, dtype=jnp.int32)[None, :]
    return ids.reshape(1, ROWS).astype(F32)


def per_device(video, assign, qkv_weight, qk_gain, text_kv, out_weight):
    sq = ("x", "y")
    core = lax.axis_index("c")
    send = pack_rows(assign, video).reshape(SQ, CAP, WIDE)
    got = lax.all_to_all(send, sq, split_axis=0, concat_axis=0, tiled=True)
    tags = got[:, :4, D : D + HALF].astype(F32).reshape(SQ, 2, SRC)
    need = jnp.transpose(tags[:, 0] * MRG + tags[:, 1])
    merged = merge_rows(got.reshape(SQ * CAP, WIDE))

    near, middle, far = gather_rows(merged)
    half_weight = lax.dynamic_slice_in_dim(out_weight, core * (D // 2), D // 2, 1)
    half_weight, middle = lax.optimization_barrier((half_weight, middle))
    own = lax.all_gather(half_weight, sq, axis=0, tiled=True)
    projected = [project(rows, qkv_weight, qk_gain) for rows in (near, middle, far)]
    queries = cat(*[q for q, _ in projected])
    kv = cat(*[kv for _, kv in projected])

    state = attend(queries, [kv], text=text_kv)
    swapped = [shift(kv, "c", 1)]
    up = down = kv
    for _ in range(3):
        up, down = shift(up, "z", 1), shift(down, "z", -1)
        state, up, down = lax.optimization_barrier((state, up, down))
        state = attend(queries, [up, down] + swapped, state)
        swapped = [shift(up, "c", 1), shift(down, "c", 1)]
    cut = ROWS // 2
    up, down = shift(up[:cut], "z", 1), shift(down[cut:], "z", -1)
    state, up, down = lax.optimization_barrier((state, up, down))
    state = attend(queries, [up, down] + swapped, state)
    swapped = [shift(up, "c", 1), shift(down, "c", 1)]
    parts = attend(queries, swapped, state, finish_with=(need, row_ids()))
    own, mark = lax.optimization_barrier((own, parts[0, :16]))
    other = shift(own, "c", 1)
    parts = lax.all_to_all(parts, sq, split_axis=0, concat_axis=0, tiled=True)
    return finish(core.astype(jnp.int32).reshape(1), parts, own, other, video, mark)


def solution(mesh):
    fine = Mesh(mesh.devices.reshape(4, 4, 8, 2), ("x", "y", "z", "c"))
    sq = ("x", "y")
    in_specs = (
        P(("x", "y", "z", "c"), None),
        P(("x", "y", "z", "c")),
        P(None, sq),
        P(),
        P(None, None, sq),
        P(sq, None),
    )
    out_specs = P(("x", "y", "z", "c"), None)
    return jax.shard_map(
        per_device, mesh=fine, in_specs=in_specs, out_specs=out_specs, check_vma=False
    )
```

```python
import functools
import math

import jax
import jax.numpy as jnp
from jax import lax
from jax.experimental import pallas as pl
from jax.experimental.pallas import tpu as pltpu
from jax.sharding import Mesh, PartitionSpec as P

BF = jnp.bfloat16
F32 = jnp.float32
HD = 128
SQ = 16
SK = 16
CAP = 24
MRG = 48
SRC = 192
ROWS = SQ * MRG
TEXT = 256
D = 3072


def dot(a, b):
    return lax.dot_general(a, b, (((1,), (0,)), ((), ())), preferred_element_type=F32)


def dot_t(a, b):
    return lax.dot_general(a, b, (((1,), (1,)), ((), ())), preferred_element_type=F32)


WIDE = D + HD
HALF = SRC // 2


def pack_kernel(row_ref, video_ref, out_ref, tags_ref):
    row = row_ref[...]
    peer = row // (MRG * SK)
    local = row % MRG
    own_peer = lax.broadcasted_iota(jnp.int32, (SQ, SRC), 0) == peer
    hot = jnp.where(own_peer, 1.0, 0.0)
    before = lax.broadcasted_iota(jnp.int32, (SRC, SRC), 0) < lax.broadcasted_iota(
        jnp.int32, (SRC, SRC), 1
    )
    ranks = dot(hot.astype(BF), jnp.where(before, 1.0, 0.0).astype(BF))
    rank = jnp.sum(hot * ranks, axis=0, keepdims=True).astype(jnp.int32)
    position = peer * CAP + rank
    chosen = lax.broadcasted_iota(jnp.int32, (SQ * CAP, SRC), 0) == position
    out_ref[:, :D] = dot(jnp.where(chosen, 1.0, 0.0).astype(BF), video_ref[...]).astype(BF)
    number = (local + 1).astype(F32)
    slot_number = jnp.sum(jnp.where(chosen, number, 0.0), axis=1, keepdims=True)
    lanes = lax.broadcasted_iota(jnp.int32, (SQ * CAP, HD), 1)
    tags_ref[...] = jnp.where(lanes == HD - 1, slot_number, 0.0)
    for slot, part in enumerate((peer, local)):
        part = part.astype(F32)
        low, high = part[:, :HALF], part[:, HALF:]
        for place in range(2 * slot, SQ * CAP, CAP):
            tags_ref[place : place + 1, :HALF] = low
            tags_ref[place + 1 : place + 2, :HALF] = high
    out_ref[:, D:] = tags_ref[...].astype(BF)


def pack_rows(assign, video):
    return pl.pallas_call(
        pack_kernel,
        out_shape=jax.ShapeDtypeStruct((SQ * CAP, WIDE), BF),
        scratch_shapes=[pltpu.VMEM((SQ * CAP, HD), F32)],
        compiler_params=pltpu.CompilerParams(vmem_limit_bytes=16 << 20),
        name="pack_rows",
    )(assign.reshape(1, SRC), video)


def merge_kernel(got_ref, out_ref):
    number = got_ref[:, WIDE - 1 :].astype(F32)
    places = lax.broadcasted_iota(jnp.int32, (SQ * CAP, MRG), 1).astype(F32) + 1.0
    member = jnp.where(number == places, 1.0, 0.0).astype(BF)

    def over_slots(values):
        return lax.dot_general(
            member, values, (((0,), (0,)), ((), ())), preferred_element_type=F32
        )

    counts = over_slots(jnp.ones((SQ * CAP, HD), BF))[:, :1]
    out_ref[...] = (over_slots(got_ref[:, :D]) / jnp.maximum(counts, 1.0)).astype(BF)


def merge_rows(got):
    return pl.pallas_call(
        merge_kernel,
        out_shape=jax.ShapeDtypeStruct((MRG, D), BF),
        compiler_params=pltpu.CompilerParams(vmem_limit_bytes=16 << 20),
        name="merge_rows",
    )(got)


def project_kernel(*refs):
    *row_refs, weight_ref, gain_ref, q_ref, kv_ref = refs

    def norm(part, gain):
        return part * lax.rsqrt(jnp.mean(part * part, axis=-1, keepdims=True) + 1e-06) * gain

    factor = math.log2(math.e) / math.sqrt(HD)
    full = dot(jnp.concatenate([ref[...] for ref in row_refs], axis=0), weight_ref[...])
    q_ref[...] = (norm(full[:, :HD], gain_ref[0:1, :]) * factor).astype(BF)
    kv_ref[:, :HD] = norm(full[:, HD : 2 * HD], gain_ref[1:2, :]).astype(BF)
    kv_ref[:, HD:] = full[:, 2 * HD :].astype(BF)


def project(pieces, weight, gain):
    count = sum(piece.shape[0] for piece in pieces)
    return pl.pallas_call(
        project_kernel,
        out_shape=[
            jax.ShapeDtypeStruct((count, HD), BF),
            jax.ShapeDtypeStruct((count, 2 * HD), BF),
        ],
        compiler_params=pltpu.CompilerParams(vmem_limit_bytes=16 << 20),
        cost_estimate=pl.CostEstimate(
            flops=2 * count * D * 3 * HD, bytes_accessed=2 * D * (count + 3 * HD), transcendentals=0
        ),
        name="project",
    )(*pieces, weight, gain)


QB = 256
CHUNK = 768


def attend_kernel(first, last, pieces, *refs):
    q_ref, *refs = refs
    text_ref = refs.pop(0) if first else None
    kv_refs = [refs.pop(0) for _ in range(pieces)]
    if not first:
        m_in, acc_in = refs.pop(0), refs.pop(0)
    if last:
        need_ref, ids_ref, out_ref, m_ref, acc_ref, wide_ref, done_ref = refs
    else:
        m_ref, acc_ref, wide_ref = refs

    wide_ref[:, HD:] = jnp.ones((wide_ref.shape[0], HD), BF)
    chunks = []
    place = 0
    if first:
        wide_ref[:TEXT, :HD] = text_ref[1]
        chunks.append((text_ref[0], 0, TEXT))
        place = TEXT
    for ref in kv_refs:
        size = ref.shape[0]
        wide_ref[place : place + size, :HD] = ref[:, HD:]
        for start in range(0, size, CHUNK):
            width = min(CHUNK, size - start)
            chunks.append((ref[start : start + width, :HD], place + start, width))
        place += size

    for index, (keys, start, width) in enumerate(chunks):
        values = wide_ref[start : start + width, :]
        fresh = first and index == 0
        from_m, from_acc = (m_in, acc_in) if index == 0 and not first else (m_ref, acc_ref)
        for block in range(ROWS // QB):
            span = pl.ds(block * QB, QB)
            scores = dot_t(q_ref[span, :], keys)
            raised = jnp.max(scores, axis=-1, keepdims=True)
            if not fresh:
                before = from_m[span, :1]
                raised = jnp.maximum(before, raised)
                fading = jnp.exp2(before - raised)
            probs = jnp.exp2(scores - raised).astype(BF)
            update = dot(probs, values)
            if not fresh:
                update = from_acc[span, :] * fading + update
            acc_ref[span, :] = update
            m_ref[span, :] = jnp.broadcast_to(raised, (QB, HD))

    if last:
        done_ref[...] = (acc_ref[:, :HD] / acc_ref[:, HD:]).astype(BF)
        for peer in range(SQ):
            wanted = need_ref[:, peer : peer + 1]
            hot = jnp.where(wanted == ids_ref[...], 1.0, 0.0).astype(BF)
            out_ref[peer] = dot(hot, done_ref[...]).astype(BF)


def attend(queries, kv, state=None, text=None, finish_with=None):
    first, last = text is not None, finish_with is not None
    keys = sum(piece.shape[0] for piece in kv) + (TEXT if first else 0)
    shapes = [(ROWS, HD), (ROWS, 2 * HD)]
    scratch = [pltpu.VMEM((keys, 2 * HD), BF)]
    operands = [queries] + ([text] if first else []) + list(kv) + ([] if first else list(state))
    if last:
        operands += list(finish_with)
        out_shape = jax.ShapeDtypeStruct((SQ, SRC, HD), BF)
        scratch = [pltpu.VMEM(shape, F32) for shape in shapes] + scratch
        scratch.append(pltpu.VMEM((ROWS, HD), BF))
    else:
        out_shape = [jax.ShapeDtypeStruct(shape, F32) for shape in shapes]
    return pl.pallas_call(
        functools.partial(attend_kernel, first, last, len(kv)),
        out_shape=out_shape,
        scratch_shapes=scratch,
        compiler_params=pltpu.CompilerParams(vmem_limit_bytes=16 << 20),
        cost_estimate=pl.CostEstimate(
            flops=6 * ROWS * keys * HD,
            bytes_accessed=4 * keys * HD,
            transcendentals=ROWS * keys,
        ),
        name="attend",
    )(*operands)


def finish_kernel(core_ref, parts_ref, own_ref, other_ref, video_ref, mark_ref, out_ref, flat_ref):
    step = pl.program_id(0)
    half = pl.num_programs(0) // 2

    @pl.when(step == 0)
    def _():
        for group in range(SQ):
            flat_ref[:, group * HD : (group + 1) * HD] = parts_ref[group]

    def product(weight_ref):
        delta = dot(flat_ref[...], weight_ref[...]).astype(BF).astype(F32)
        out_ref[...] = (video_ref[...].astype(F32) + delta).astype(BF)

    @pl.when(step < half)
    def _():
        product(own_ref)

    @pl.when(step >= half)
    def _():
        product(other_ref)


def finish(core, parts, own, other, video, mark):
    width = 512
    half = D // 2 // width

    def place(step, core_ref):
        return (0, lax.rem(step + half * core_ref[0], 2 * half))

    return pl.pallas_call(
        finish_kernel,
        grid_spec=pltpu.PrefetchScalarGridSpec(
            num_scalar_prefetch=1,
            grid=(2 * half,),
            in_specs=[
                pl.BlockSpec((SQ, SRC, HD), lambda c, core_ref: (0, 0, 0)),
                pl.BlockSpec((SQ * HD, width), lambda c, core_ref: (0, jnp.minimum(c, half - 1))),
                pl.BlockSpec((SQ * HD, width), lambda c, core_ref: (0, jnp.maximum(c - half, 0))),
                pl.BlockSpec((SRC, width), place),
                pl.BlockSpec((16, HD), lambda c, core_ref: (0, 0)),
            ],
            out_specs=pl.BlockSpec((SRC, width), place),
            scratch_shapes=[pltpu.VMEM((SRC, SQ * HD), BF)],
        ),
        out_shape=jax.ShapeDtypeStruct((SRC, D), BF),
        compiler_params=pltpu.CompilerParams(vmem_limit_bytes=20 << 20),
        name="finish",
    )(core, parts, own, other, video, mark)


SIZE = {"x": 4, "y": 4, "z": 8, "c": 2}


def shift(value, axis, by):
    size = SIZE[axis]
    return lax.ppermute(value, axis, [(i, (i + by) % size) for i in range(size)])


def cat(*pieces):
    return jnp.concatenate(pieces, axis=0)


def far_shift(up, down, axis, core):
    size = SIZE[axis]
    pairs = []
    for i in range(size):
        pairs.append((2 * i, 2 * ((i + 1) % size)))
        pairs.append((2 * i + 1, 2 * ((i - 1) % size) + 1))
    return lax.ppermute(jnp.where(core == 0, up, down), (axis, "c"), pairs)


def gather_rows(merged, core, project_set, later):
    half = MRG // 2
    a, b = merged[:half], merged[half:]
    a_near = [shift(a, "x", k) for k in (1, -1, 2)]
    b_near = [shift(b, "y", k) for k in (1, -1, 2)]
    a_line, b_line = cat(a, *a_near), cat(b, *b_near)
    a_up, a_down = shift(a_line, "y", 1), shift(a_line, "y", -1)
    b_up, b_down = shift(b_line, "x", 1), shift(b_line, "x", -1)
    near = project_set([a_line, b_line])
    near, a_up, a_down, later = lax.optimization_barrier((near, a_up, a_down, later))
    a_far = far_shift(a_up, a_down, "y", core)
    near, b_up, b_down = lax.optimization_barrier((near, b_up, b_down))
    b_far = far_shift(b_up, b_down, "x", core)
    middle = project_set([a_up, a_down, b_up, b_down])
    far = project_set([a_far, b_far])
    return near, middle, far, later


def row_ids():
    x, y = lax.axis_index("x"), lax.axis_index("y")
    near = (0, -1, 1, 2)
    places = [(k, 0, 0) for k in near] + [(0, k, 1) for k in near]
    places += [(k, -1, 0) for k in near] + [(k, 1, 0) for k in near]
    places += [(-1, k, 1) for k in near] + [(1, k, 1) for k in near]
    places += [(k, 2, 0) for k in near] + [(2, k, 1) for k in near]
    dx, dy, part = (jnp.array(column, jnp.int32) for column in zip(*places))
    owner = (x + dx) % 4 * 4 + (y + dy) % 4
    half = MRG // 2
    ids = (owner * MRG + part * half)[:, None] + jnp.arange(half, dtype=jnp.int32)[None, :]
    return ids.reshape(1, ROWS).astype(F32)


def per_device(video, assign, qkv_weight, qk_gain, text_kv, out_weight):
    sq = ("x", "y")
    core = lax.axis_index("c")
    send = pack_rows(assign, video).reshape(SQ, CAP, WIDE)
    got = lax.all_to_all(send, sq, split_axis=0, concat_axis=0, tiled=True)
    tags = got[:, :4, D : D + HALF].astype(F32).reshape(SQ, 2, SRC)
    need = jnp.transpose(tags[:, 0] * MRG + tags[:, 1])
    merged = merge_rows(got.reshape(SQ * CAP, WIDE))

    half_weight = lax.dynamic_slice_in_dim(out_weight, core * (D // 2), D // 2, 1)
    near, middle, far, half_weight = gather_rows(
        merged, core, lambda rows: project(rows, qkv_weight, qk_gain), half_weight
    )
    own = lax.all_gather(half_weight, sq, axis=0, tiled=True)
    queries, kv = (cat(*pieces) for pieces in zip(near, middle, far))

    state = attend(queries, [kv], text=text_kv)
    swapped = [shift(kv, "c", 1)]
    up = down = kv
    for _ in range(3):
        up, down = shift(up, "z", 1), shift(down, "z", -1)
        state, up, down = lax.optimization_barrier((state, up, down))
        state = attend(queries, [up, down] + swapped, state)
        swapped = [shift(up, "c", 1), shift(down, "c", 1)]
    last = far_shift(up, down, "z", core)
    state, last = lax.optimization_barrier((state, last))
    state = attend(queries, [last] + swapped, state)
    swapped = [shift(last, "c", 1)]
    parts = attend(queries, swapped, state, finish_with=(need, row_ids()))
    own, mark = lax.optimization_barrier((own, parts[0, :16]))
    other = shift(own, "c", 1)
    parts = lax.all_to_all(parts, sq, split_axis=0, concat_axis=0, tiled=True)
    return finish(core.astype(jnp.int32).reshape(1), parts, own, other, video, mark)


def solution(mesh):
    fine = Mesh(mesh.devices.reshape(4, 4, 8, 2), ("x", "y", "z", "c"))
    sq = ("x", "y")
    in_specs = (
        P(("x", "y", "z", "c"), None),
        P(("x", "y", "z", "c")),
        P(None, sq),
        P(),
        P(None, None, sq),
        P(sq, None),
    )
    out_specs = P(("x", "y", "z", "c"), None)
    return jax.shard_map(
        per_device, mesh=fine, in_specs=in_specs, out_specs=out_specs, check_vma=False
    )
```

```python
import functools
import math

import jax
import jax.numpy as jnp
from jax import lax
from jax.experimental import pallas as pl
from jax.experimental.pallas import tpu as pltpu
from jax.sharding import Mesh, PartitionSpec as P

BF = jnp.bfloat16
F32 = jnp.float32
HD = 128
SQ = 16
SK = 16
CAP = 24
MRG = 48
SRC = 192
ROWS = SQ * MRG
TEXT = 256
D = 3072


def dot(a, b):
    return lax.dot_general(a, b, (((1,), (0,)), ((), ())), preferred_element_type=F32)


def dot_t(a, b):
    return lax.dot_general(a, b, (((1,), (1,)), ((), ())), preferred_element_type=F32)


WIDE = D + HD
HALF = SRC // 2


def pack_kernel(row_ref, video_ref, out_ref, tags_ref):
    row = row_ref[...]
    peer = row // (MRG * SK)
    local = row % MRG
    own_peer = lax.broadcasted_iota(jnp.int32, (SQ, SRC), 0) == peer
    hot = jnp.where(own_peer, 1.0, 0.0)
    before = lax.broadcasted_iota(jnp.int32, (SRC, SRC), 0) < lax.broadcasted_iota(
        jnp.int32, (SRC, SRC), 1
    )
    ranks = dot(hot.astype(BF), jnp.where(before, 1.0, 0.0).astype(BF))
    rank = jnp.sum(hot * ranks, axis=0, keepdims=True).astype(jnp.int32)
    position = peer * CAP + rank
    chosen = lax.broadcasted_iota(jnp.int32, (SQ * CAP, SRC), 0) == position
    out_ref[:, :D] = dot(jnp.where(chosen, 1.0, 0.0).astype(BF), video_ref[...]).astype(BF)
    number = (local + 1).astype(F32)
    slot_number = jnp.sum(jnp.where(chosen, number, 0.0), axis=1, keepdims=True)
    lanes = lax.broadcasted_iota(jnp.int32, (SQ * CAP, HD), 1)
    tags_ref[...] = jnp.where(lanes == HD - 1, slot_number, 0.0)
    for slot, part in enumerate((peer, local)):
        part = part.astype(F32)
        low, high = part[:, :HALF], part[:, HALF:]
        for place in range(2 * slot, SQ * CAP, CAP):
            tags_ref[place : place + 1, :HALF] = low
            tags_ref[place + 1 : place + 2, :HALF] = high
    out_ref[:, D:] = tags_ref[...].astype(BF)


def pack_rows(assign, video):
    return pl.pallas_call(
        pack_kernel,
        out_shape=jax.ShapeDtypeStruct((SQ * CAP, WIDE), BF),
        scratch_shapes=[pltpu.VMEM((SQ * CAP, HD), F32)],
        compiler_params=pltpu.CompilerParams(vmem_limit_bytes=16 << 20),
        name="pack_rows",
    )(assign.reshape(1, SRC), video)


def merge_kernel(got_ref, low_ref, high_ref, need_ref, tags_ref, flat_ref):
    tags_ref[...] = got_ref[:, D:].astype(F32)
    number = tags_ref[:, HD - 1 :]
    places = lax.broadcasted_iota(jnp.int32, (SQ * CAP, MRG), 1).astype(F32) + 1.0
    member = jnp.where(number == places, 1.0, 0.0).astype(BF)

    def over_slots(values):
        return lax.dot_general(
            member, values, (((0,), (0,)), ((), ())), preferred_element_type=F32
        )

    counts = over_slots(jnp.ones((SQ * CAP, HD), BF))[:, :1]
    merged = over_slots(got_ref[:, :D]) / jnp.maximum(counts, 1.0)
    low_ref[...] = merged[: MRG // 2].astype(BF)
    high_ref[...] = merged[MRG // 2 :].astype(BF)
    flat_ref[...] = jnp.zeros_like(flat_ref)
    for peer in range(SQ):
        for part in range(2):
            row = peer * CAP + part
            owner, local = tags_ref[row : row + 1, :HALF], tags_ref[row + 2 : row + 3, :HALF]
            flat_ref[peer : peer + 1, part * HALF : (part + 1) * HALF] = owner * MRG + local
    need_ref[...] = jnp.transpose(flat_ref[...])


def merge_rows(got):
    half = jax.ShapeDtypeStruct((MRG // 2, D), BF)
    return pl.pallas_call(
        merge_kernel,
        out_shape=[half, half, jax.ShapeDtypeStruct((2 * HD, HD), F32)],
        scratch_shapes=[pltpu.VMEM((SQ * CAP, HD), F32), pltpu.VMEM((HD, 2 * HD), F32)],
        compiler_params=pltpu.CompilerParams(vmem_limit_bytes=16 << 20),
        name="merge_rows",
    )(got)


def join_kernel(*refs):
    *parts, out_ref = refs
    out_ref[...] = jnp.concatenate([ref[...] for ref in parts], axis=0)


def join(*parts):
    rows = sum(part.shape[0] for part in parts)
    return pl.pallas_call(
        join_kernel,
        out_shape=jax.ShapeDtypeStruct((rows, parts[0].shape[1]), BF),
        compiler_params=pltpu.CompilerParams(vmem_limit_bytes=16 << 20),
        name="join",
    )(*parts)


def project_kernel(*refs):
    *row_refs, weight_ref, gain_ref, q_ref, kv_ref = refs

    def norm(part, gain):
        return part * lax.rsqrt(jnp.mean(part * part, axis=-1, keepdims=True) + 1e-06) * gain

    factor = math.log2(math.e) / math.sqrt(HD)
    full = dot(jnp.concatenate([ref[...] for ref in row_refs], axis=0), weight_ref[...])
    q_ref[...] = (norm(full[:, :HD], gain_ref[0:1, :]) * factor).astype(BF)
    kv_ref[:, :HD] = norm(full[:, HD : 2 * HD], gain_ref[1:2, :]).astype(BF)
    kv_ref[:, HD:] = full[:, 2 * HD :].astype(BF)


def project(pieces, weight, gain):
    count = sum(piece.shape[0] for piece in pieces)
    return pl.pallas_call(
        project_kernel,
        out_shape=[
            jax.ShapeDtypeStruct((count, HD), BF),
            jax.ShapeDtypeStruct((count, 2 * HD), BF),
        ],
        compiler_params=pltpu.CompilerParams(vmem_limit_bytes=16 << 20),
        cost_estimate=pl.CostEstimate(
            flops=2 * count * D * 3 * HD, bytes_accessed=2 * D * (count + 3 * HD), transcendentals=0
        ),
        name="project",
    )(*pieces, weight, gain)


QB = 256
CHUNK = 768


def attend_kernel(first, last, pieces, *refs):
    q_ref, *refs = refs
    text_ref = refs.pop(0) if first else None
    kv_refs = [refs.pop(0) for _ in range(pieces)]
    if not first:
        m_in, acc_in = refs.pop(0), refs.pop(0)
    if last:
        need_ref, ids_ref, out_ref, m_ref, acc_ref, wide_ref, done_ref = refs
    else:
        m_ref, acc_ref, wide_ref = refs

    wide_ref[:, HD:] = jnp.ones((wide_ref.shape[0], HD), BF)
    chunks = []
    place = 0
    if first:
        wide_ref[:TEXT, :HD] = text_ref[1]
        chunks.append((text_ref[0], 0, TEXT))
        place = TEXT
    for ref in kv_refs:
        size = ref.shape[0]
        wide_ref[place : place + size, :HD] = ref[:, HD:]
        for start in range(0, size, CHUNK):
            width = min(CHUNK, size - start)
            chunks.append((ref[start : start + width, :HD], place + start, width))
        place += size

    for index, (keys, start, width) in enumerate(chunks):
        values = wide_ref[start : start + width, :]
        fresh = first and index == 0
        from_m, from_acc = (m_in, acc_in) if index == 0 and not first else (m_ref, acc_ref)
        for block in range(ROWS // QB):
            span = pl.ds(block * QB, QB)
            scores = dot_t(q_ref[span, :], keys)
            raised = jnp.max(scores, axis=-1, keepdims=True)
            if not fresh:
                before = from_m[span, :1]
                raised = jnp.maximum(before, raised)
                fading = jnp.exp2(before - raised)
            probs = jnp.exp2(scores - raised).astype(BF)
            update = dot(probs, values)
            if not fresh:
                update = from_acc[span, :] * fading + update
            acc_ref[span, :] = update
            m_ref[span, :] = jnp.broadcast_to(raised, (QB, HD))

    if last:
        done_ref[...] = (acc_ref[:, :HD] / acc_ref[:, HD:]).astype(BF)
        for peer in range(SQ):
            wanted = need_ref[:SRC, peer : peer + 1]
            hot = jnp.where(wanted == ids_ref[...], 1.0, 0.0).astype(BF)
            out_ref[peer] = dot(hot, done_ref[...]).astype(BF)


def attend(queries, kv, state=None, text=None, finish_with=None):
    first, last = text is not None, finish_with is not None
    keys = sum(piece.shape[0] for piece in kv) + (TEXT if first else 0)
    shapes = [(ROWS, HD), (ROWS, 2 * HD)]
    scratch = [pltpu.VMEM((keys, 2 * HD), BF)]
    operands = [queries] + ([text] if first else []) + list(kv) + ([] if first else list(state))
    if last:
        operands += list(finish_with)
        out_shape = jax.ShapeDtypeStruct((SQ, SRC, HD), BF)
        scratch = [pltpu.VMEM(shape, F32) for shape in shapes] + scratch
        scratch.append(pltpu.VMEM((ROWS, HD), BF))
    else:
        out_shape = [jax.ShapeDtypeStruct(shape, F32) for shape in shapes]
    return pl.pallas_call(
        functools.partial(attend_kernel, first, last, len(kv)),
        out_shape=out_shape,
        input_output_aliases={} if first or last else {len(kv) + 1: 0, len(kv) + 2: 1},
        scratch_shapes=scratch,
        compiler_params=pltpu.CompilerParams(vmem_limit_bytes=16 << 20),
        cost_estimate=pl.CostEstimate(
            flops=6 * ROWS * keys * HD,
            bytes_accessed=4 * keys * HD,
            transcendentals=ROWS * keys,
        ),
        name="attend",
    )(*operands)


WIDTH = 512


def finish_kernel(
    core_ref, parts_ref, swapped_ref, weight_hbm, video_ref, out_ref, sent_ref, flat_ref, weight_ref, sems
):
    step = pl.program_id(0)

    def copy(index):
        columns = pl.ds(pl.multiple_of(index * WIDTH, WIDTH), WIDTH)
        return pltpu.make_async_copy(
            weight_hbm.at[:, columns], weight_ref.at[index], sems.at[index]
        )

    @pl.when(step == 0)
    def _():
        for index in range(D // 2 // WIDTH):
            copy(index).start()
        for group in range(SQ):
            flat_ref[:SRC, group * HD : (group + 1) * HD] = parts_ref[group]
            flat_ref[SRC:, group * HD : (group + 1) * HD] = swapped_ref[group]

    copy(step).wait()
    delta = dot(flat_ref[...], weight_ref[step]).astype(BF)
    sent_ref[...] = delta[SRC:]
    out_ref[...] = (video_ref[...].astype(F32) + delta[:SRC].astype(F32)).astype(BF)


def finish(core, parts, swapped, weight, video):
    steps = D // 2 // WIDTH

    def own_place(step, core_ref):
        return (0, step + steps * core_ref[0])

    whole = pl.BlockSpec((SQ, SRC, HD), lambda c, core_ref: (0, 0, 0))
    return pl.pallas_call(
        finish_kernel,
        grid_spec=pltpu.PrefetchScalarGridSpec(
            num_scalar_prefetch=1,
            grid=(steps,),
            in_specs=[
                whole,
                whole,
                pl.BlockSpec(memory_space=pltpu.HBM),
                pl.BlockSpec((SRC, WIDTH), own_place),
            ],
            out_specs=[
                pl.BlockSpec((SRC, WIDTH), own_place),
                pl.BlockSpec((SRC, WIDTH), lambda c, core_ref: (0, c)),
            ],
            scratch_shapes=[
                pltpu.VMEM((2 * SRC, SQ * HD), BF),
                pltpu.VMEM((steps, SQ * HD, WIDTH), BF),
                pltpu.SemaphoreType.DMA((steps,)),
            ],
        ),
        out_shape=[
            jax.ShapeDtypeStruct((SRC, D), BF),
            jax.ShapeDtypeStruct((SRC, D // 2), BF),
        ],
        compiler_params=pltpu.CompilerParams(vmem_limit_bytes=60 << 20),
        name="finish",
    )(core, parts, swapped, weight, video)


def place_kernel(core_ref, half_ref, delta_ref, video_ref, out_ref):
    out_ref[...] = (video_ref[...].astype(F32) + delta_ref[...].astype(F32)).astype(BF)


def place(core, half, delta, video):
    width = 768
    steps = D // 2 // width

    def other_place(step, core_ref):
        return (0, step + steps * (1 - core_ref[0]))

    return pl.pallas_call(
        place_kernel,
        grid_spec=pltpu.PrefetchScalarGridSpec(
            num_scalar_prefetch=1,
            grid=(steps,),
            in_specs=[
                pl.BlockSpec(memory_space=pl.ANY),
                pl.BlockSpec((SRC, width), lambda c, core_ref: (0, c)),
                pl.BlockSpec((SRC, width), other_place),
            ],
            out_specs=pl.BlockSpec((SRC, width), other_place),
        ),
        out_shape=jax.ShapeDtypeStruct((SRC, D), BF),
        input_output_aliases={1: 0},
        compiler_params=pltpu.CompilerParams(vmem_limit_bytes=16 << 20),
        name="place",
    )(core, half, delta, video)


SIZE = {"x": 4, "y": 4, "z": 8, "c": 2}


def shift(value, axis, by):
    size = SIZE[axis]
    return lax.ppermute(value, axis, [(i, (i + by) % size) for i in range(size)])


def cat(*pieces):
    return jnp.concatenate(pieces, axis=0)


def pick_kernel(core_ref, first_ref, second_ref, out_ref):
    @pl.when(core_ref[0] == 0)
    def _():
        out_ref[...] = first_ref[...]

    @pl.when(core_ref[0] != 0)
    def _():
        out_ref[...] = second_ref[...]


def pick(core, first, second):
    return pl.pallas_call(
        pick_kernel,
        in_specs=[
            pl.BlockSpec(memory_space=pltpu.SMEM),
            pl.BlockSpec(memory_space=pltpu.VMEM),
            pl.BlockSpec(memory_space=pltpu.VMEM),
        ],
        out_shape=jax.ShapeDtypeStruct(first.shape, first.dtype),
        compiler_params=pltpu.CompilerParams(vmem_limit_bytes=16 << 20),
        name="pick",
    )(core, first, second)


def far_shift(up, down, axis, core):
    size = SIZE[axis]
    pairs = []
    for i in range(size):
        pairs.append((2 * i, 2 * ((i + 1) % size)))
        pairs.append((2 * i + 1, 2 * ((i - 1) % size) + 1))
    return lax.ppermute(pick(core, up, down), (axis, "c"), pairs)


def gather_rows(a, b, core, project_set, later):
    a_near = [shift(a, "x", k) for k in (1, -1, 2)]
    b_near = [shift(b, "y", k) for k in (1, -1, 2)]
    a_line, b_line = join(a, *a_near), join(b, *b_near)
    around = [shift(a_line, "y", 1), shift(a_line, "y", -1)]
    around += [shift(b_line, "x", 1), shift(b_line, "x", -1)]
    near = project_set([a_line, b_line])
    near, around, later = lax.optimization_barrier((near, around, later))
    far = [far_shift(*around[:2], "y", core), far_shift(*around[2:], "x", core)]
    middle = project_set(around)
    return near, middle, project_set(far), later


def row_ids():
    x, y = lax.axis_index("x"), lax.axis_index("y")
    near = (0, -1, 1, 2)
    places = [(k, 0, 0) for k in near] + [(0, k, 1) for k in near]
    places += [(k, -1, 0) for k in near] + [(k, 1, 0) for k in near]
    places += [(-1, k, 1) for k in near] + [(1, k, 1) for k in near]
    places += [(k, 2, 0) for k in near] + [(2, k, 1) for k in near]
    dx, dy, part = (jnp.array(column, jnp.int32) for column in zip(*places))
    owner = (x + dx) % 4 * 4 + (y + dy) % 4
    half = MRG // 2
    ids = (owner * MRG + part * half)[:, None] + jnp.arange(half, dtype=jnp.int32)[None, :]
    return ids.reshape(1, ROWS).astype(F32)


def per_device(video, assign, qkv_weight, qk_gain, text_kv, out_weight):
    sq = ("x", "y")
    core = lax.axis_index("c").astype(jnp.int32)
    send = pack_rows(assign, video).reshape(SQ, CAP, WIDE)
    got = lax.all_to_all(send, sq, split_axis=0, concat_axis=0, tiled=True)
    low, high, need = merge_rows(got.reshape(SQ * CAP, WIDE))

    half_weight = lax.dynamic_slice_in_dim(out_weight, core * (D // 2), D // 2, 1)
    core = core.reshape(1)
    near, middle, far, half_weight = gather_rows(
        low, high, core, lambda rows: project(rows, qkv_weight, qk_gain), half_weight
    )
    own = lax.all_gather(half_weight, sq, axis=0, tiled=True)
    queries, kv = (cat(*pieces) for pieces in zip(near, middle, far))

    state = attend(queries, [kv], text=text_kv)
    swapped = [shift(kv, "c", 1)]
    up = down = kv
    for _ in range(3):
        up, down = shift(up, "z", 1), shift(down, "z", -1)
        state, up, down = lax.optimization_barrier((state, up, down))
        state = attend(queries, [up, down] + swapped, state)
        swapped = [shift(up, "c", 1), shift(down, "c", 1)]
    last = far_shift(up, down, "z", core)
    state, last = lax.optimization_barrier((state, last))
    state = attend(queries, [last] + swapped, state)
    swapped = [shift(last, "c", 1)]
    parts = attend(queries, swapped, state, finish_with=(need, row_ids()))
    parts = lax.all_to_all(parts, sq, split_axis=0, concat_axis=0, tiled=True)
    result, sent = finish(core, parts, shift(parts, "c", 1), own, video)
    return place(core, result, shift(sent, "c", 1), video)


def solution(mesh):
    fine = Mesh(mesh.devices.reshape(4, 4, 8, 2), ("x", "y", "z", "c"))
    sq = ("x", "y")
    in_specs = (
        P(("x", "y", "z", "c"), None),
        P(("x", "y", "z", "c")),
        P(None, sq),
        P(),
        P(None, None, sq),
        P(sq, None),
    )
    out_specs = P(("x", "y", "z", "c"), None)
    return jax.shard_map(
        per_device, mesh=fine, in_specs=in_specs, out_specs=out_specs, check_vma=False
    )
```

```python
import functools
import math

import jax
import jax.numpy as jnp
from jax import lax
from jax.experimental import pallas as pl
from jax.experimental.pallas import tpu as pltpu
from jax.sharding import Mesh, PartitionSpec as P

BF = jnp.bfloat16
F32 = jnp.float32
HD = 128
SQ = 16
SK = 16
CAP = 24
MRG = 48
SRC = 192
ROWS = SQ * MRG
TEXT = 256
D = 3072


def dot(a, b):
    return lax.dot_general(a, b, (((1,), (0,)), ((), ())), preferred_element_type=F32)


def dot_t(a, b):
    return lax.dot_general(a, b, (((1,), (1,)), ((), ())), preferred_element_type=F32)


WIDE = D + HD
HALF = SRC // 2


def pack_kernel(row_ref, video_ref, out_ref, tags_ref):
    row = row_ref[...]
    peer = row // (MRG * SK)
    local = row % MRG
    own_peer = lax.broadcasted_iota(jnp.int32, (SQ, SRC), 0) == peer
    hot = jnp.where(own_peer, 1.0, 0.0)
    before = lax.broadcasted_iota(jnp.int32, (SRC, SRC), 0) < lax.broadcasted_iota(
        jnp.int32, (SRC, SRC), 1
    )
    ranks = dot(hot.astype(BF), jnp.where(before, 1.0, 0.0).astype(BF))
    rank = jnp.sum(hot * ranks, axis=0, keepdims=True).astype(jnp.int32)
    position = peer * CAP + rank
    chosen = lax.broadcasted_iota(jnp.int32, (SQ * CAP, SRC), 0) == position
    out_ref[:, :D] = dot(jnp.where(chosen, 1.0, 0.0).astype(BF), video_ref[...]).astype(BF)
    number = (local + 1).astype(F32)
    slot_number = jnp.sum(jnp.where(chosen, number, 0.0), axis=1, keepdims=True)
    lanes = lax.broadcasted_iota(jnp.int32, (SQ * CAP, HD), 1)
    tags_ref[...] = jnp.where(lanes == HD - 1, slot_number, 0.0)
    for slot, part in enumerate((peer, local)):
        part = part.astype(F32)
        low, high = part[:, :HALF], part[:, HALF:]
        for place in range(2 * slot, SQ * CAP, CAP):
            tags_ref[place : place + 1, :HALF] = low
            tags_ref[place + 1 : place + 2, :HALF] = high
    out_ref[:, D:] = tags_ref[...].astype(BF)


def pack_rows(assign, video):
    return pl.pallas_call(
        pack_kernel,
        out_shape=jax.ShapeDtypeStruct((SQ * CAP, WIDE), BF),
        scratch_shapes=[pltpu.VMEM((SQ * CAP, HD), F32)],
        compiler_params=pltpu.CompilerParams(vmem_limit_bytes=16 << 20),
        name="pack_rows",
    )(assign.reshape(1, SRC), video)


def merge_kernel(got_ref, low_ref, high_ref, need_ref, tags_ref, flat_ref):
    tags_ref[...] = got_ref[:, D:].astype(F32)
    number = tags_ref[:, HD - 1 :]
    places = lax.broadcasted_iota(jnp.int32, (SQ * CAP, MRG), 1).astype(F32) + 1.0
    member = jnp.where(number == places, 1.0, 0.0).astype(BF)

    def over_slots(values):
        return lax.dot_general(
            member, values, (((0,), (0,)), ((), ())), preferred_element_type=F32
        )

    counts = over_slots(jnp.ones((SQ * CAP, HD), BF))[:, :1]
    merged = over_slots(got_ref[:, :D]) / jnp.maximum(counts, 1.0)
    low_ref[...] = merged[: MRG // 2].astype(BF)
    high_ref[...] = merged[MRG // 2 :].astype(BF)
    flat_ref[...] = jnp.zeros_like(flat_ref)
    for peer in range(SQ):
        for part in range(2):
            row = peer * CAP + part
            owner, local = tags_ref[row : row + 1, :HALF], tags_ref[row + 2 : row + 3, :HALF]
            flat_ref[peer : peer + 1, part * HALF : (part + 1) * HALF] = owner * MRG + local
    need_ref[...] = jnp.transpose(flat_ref[...])


def merge_rows(got):
    half = jax.ShapeDtypeStruct((MRG // 2, D), BF)
    return pl.pallas_call(
        merge_kernel,
        out_shape=[half, half, jax.ShapeDtypeStruct((2 * HD, HD), F32)],
        scratch_shapes=[pltpu.VMEM((SQ * CAP, HD), F32), pltpu.VMEM((HD, 2 * HD), F32)],
        compiler_params=pltpu.CompilerParams(vmem_limit_bytes=16 << 20),
        name="merge_rows",
    )(got)


def join_kernel(*refs):
    *parts, out_ref = refs
    out_ref[...] = jnp.concatenate([ref[...] for ref in parts], axis=0)


def join(*parts):
    rows = sum(part.shape[0] for part in parts)
    return pl.pallas_call(
        join_kernel,
        out_shape=jax.ShapeDtypeStruct((rows, parts[0].shape[1]), BF),
        compiler_params=pltpu.CompilerParams(vmem_limit_bytes=16 << 20),
        name="join",
    )(*parts)


def project_kernel(*refs):
    *row_refs, weight_ref, gain_ref, q_ref, kv_ref = refs

    def norm(part, gain):
        return part * lax.rsqrt(jnp.mean(part * part, axis=-1, keepdims=True) + 1e-06) * gain

    factor = math.log2(math.e) / math.sqrt(HD)
    full = dot(jnp.concatenate([ref[...] for ref in row_refs], axis=0), weight_ref[...])
    q_ref[...] = (norm(full[:, :HD], gain_ref[0:1, :]) * factor).astype(BF)
    kv_ref[:, :HD] = norm(full[:, HD : 2 * HD], gain_ref[1:2, :]).astype(BF)
    kv_ref[:, HD:] = full[:, 2 * HD :].astype(BF)


def project(pieces, weight, gain):
    count = sum(piece.shape[0] for piece in pieces)
    return pl.pallas_call(
        project_kernel,
        out_shape=[
            jax.ShapeDtypeStruct((count, HD), BF),
            jax.ShapeDtypeStruct((count, 2 * HD), BF),
        ],
        compiler_params=pltpu.CompilerParams(vmem_limit_bytes=16 << 20),
        cost_estimate=pl.CostEstimate(
            flops=2 * count * D * 3 * HD, bytes_accessed=2 * D * (count + 3 * HD), transcendentals=0
        ),
        name="project",
    )(*pieces, weight, gain)


QB = 256
CHUNK = 768


def attend_kernel(first, last, pieces, *refs):
    q_ref, *refs = refs
    text_ref = refs.pop(0) if first else None
    kv_refs = [refs.pop(0) for _ in range(pieces)]
    if not first:
        m_in, acc_in = refs.pop(0), refs.pop(0)
    if last:
        need_ref, ids_ref, out_ref, m_ref, acc_ref, wide_ref, done_ref = refs
    else:
        m_ref, acc_ref, wide_ref = refs

    wide_ref[:, HD:] = jnp.ones((wide_ref.shape[0], HD), BF)
    chunks = []
    place = 0
    if first:
        wide_ref[:TEXT, :HD] = text_ref[1]
        chunks.append((text_ref[0], 0, TEXT))
        place = TEXT
    for ref in kv_refs:
        size = ref.shape[0]
        wide_ref[place : place + size, :HD] = ref[:, HD:]
        for start in range(0, size, CHUNK):
            width = min(CHUNK, size - start)
            chunks.append((ref[start : start + width, :HD], place + start, width))
        place += size

    for index, (keys, start, width) in enumerate(chunks):
        values = wide_ref[start : start + width, :]
        fresh = first and index == 0
        from_m, from_acc = (m_in, acc_in) if index == 0 and not first else (m_ref, acc_ref)
        for block in range(ROWS // QB):
            span = pl.ds(block * QB, QB)
            scores = dot_t(q_ref[span, :], keys)
            raised = jnp.max(scores, axis=-1, keepdims=True)
            if not fresh:
                before = from_m[span, :1]
                raised = jnp.maximum(before, raised)
                fading = jnp.exp2(before - raised)
            probs = jnp.exp2(scores - raised).astype(BF)
            update = dot(probs, values)
            if not fresh:
                update = from_acc[span, :] * fading + update
            acc_ref[span, :] = update
            m_ref[span, :] = jnp.broadcast_to(raised, (QB, HD))

    if last:
        done_ref[...] = (acc_ref[:, :HD] / acc_ref[:, HD:]).astype(BF)
        for peer in range(SQ):
            wanted = need_ref[:SRC, peer : peer + 1]
            hot = jnp.where(wanted == ids_ref[...], 1.0, 0.0).astype(BF)
            out_ref[peer] = dot(hot, done_ref[...]).astype(BF)


def attend(queries, kv, state=None, text=None, finish_with=None):
    first, last = text is not None, finish_with is not None
    keys = sum(piece.shape[0] for piece in kv) + (TEXT if first else 0)
    shapes = [(ROWS, HD), (ROWS, 2 * HD)]
    scratch = [pltpu.VMEM((keys, 2 * HD), BF)]
    operands = [queries] + ([text] if first else []) + list(kv) + ([] if first else list(state))
    if last:
        operands += list(finish_with)
        out_shape = jax.ShapeDtypeStruct((SQ, SRC, HD), BF)
        scratch = [pltpu.VMEM(shape, F32) for shape in shapes] + scratch
        scratch.append(pltpu.VMEM((ROWS, HD), BF))
    else:
        out_shape = [jax.ShapeDtypeStruct(shape, F32) for shape in shapes]
    return pl.pallas_call(
        functools.partial(attend_kernel, first, last, len(kv)),
        out_shape=out_shape,
        input_output_aliases={} if first or last else {len(kv) + 1: 0, len(kv) + 2: 1},
        scratch_shapes=scratch,
        compiler_params=pltpu.CompilerParams(vmem_limit_bytes=16 << 20),
        cost_estimate=pl.CostEstimate(
            flops=6 * ROWS * keys * HD,
            bytes_accessed=4 * keys * HD,
            transcendentals=ROWS * keys,
        ),
        name="attend",
    )(*operands)


STRIPS = 4


def flatten(parts_ref, flat_ref):
    for group in range(SQ):
        flat_ref[:, group * HD : (group + 1) * HD] = parts_ref[group]


def half_columns(index):
    return pl.ds(pl.multiple_of(index * (D // 2), D // 2), D // 2)


def own_kernel(core_ref, parts_ref, weight_hbm, video_ref, out_ref, weight_ref, flat_ref, sums_ref, sems):
    rows = SQ * HD // STRIPS

    def copy(strip):
        span = pl.ds(strip * rows, rows)
        return pltpu.make_async_copy(weight_hbm.at[span], weight_ref.at[span], sems.at[strip])

    for strip in range(STRIPS):
        copy(strip).start()
    flatten(parts_ref, flat_ref)
    for strip in range(STRIPS):
        copy(strip).wait()
        span = slice(strip * rows, (strip + 1) * rows)
        term = dot(flat_ref[:, span], weight_ref[span, :])
        if strip > 0:
            term = sums_ref[...] + term
        if strip < STRIPS - 1:
            sums_ref[...] = term
    delta = term.astype(BF).astype(F32)
    columns = half_columns(core_ref[0])
    out_ref[:, columns] = (video_ref[:, columns].astype(F32) + delta).astype(BF)


def finish_own(core, parts, weight, video):
    vmem = pl.BlockSpec(memory_space=pltpu.VMEM)
    return pl.pallas_call(
        own_kernel,
        in_specs=[
            pl.BlockSpec(memory_space=pltpu.SMEM),
            vmem,
            pl.BlockSpec(memory_space=pltpu.HBM),
            vmem,
        ],
        out_specs=[vmem, vmem],
        out_shape=[
            jax.ShapeDtypeStruct((SRC, D), BF),
            pltpu.VMEM((SQ * HD, D // 2), BF),
        ],
        scratch_shapes=[
            pltpu.VMEM((SRC, SQ * HD), BF),
            pltpu.VMEM((SRC, D // 2), F32),
            pltpu.SemaphoreType.DMA((STRIPS,)),
        ],
        compiler_params=pltpu.CompilerParams(vmem_limit_bytes=44 << 20),
        cost_estimate=pl.CostEstimate(
            flops=SRC * SQ * HD * D, bytes_accessed=SQ * HD * D, transcendentals=0
        ),
        name="finish_own",
    )(core, parts, weight, video)


def swapped_kernel(parts_ref, weight_ref, out_ref, flat_ref):
    flatten(parts_ref, flat_ref)
    out_ref[...] = dot(flat_ref[...], weight_ref[...]).astype(BF)


def finish_swapped(parts, weight):
    return pl.pallas_call(
        swapped_kernel,
        out_shape=jax.ShapeDtypeStruct((SRC, D // 2), BF),
        scratch_shapes=[pltpu.VMEM((SRC, SQ * HD), BF)],
        compiler_params=pltpu.CompilerParams(vmem_limit_bytes=16 << 20),
        cost_estimate=pl.CostEstimate(
            flops=SRC * SQ * HD * D, bytes_accessed=SQ * HD * D, transcendentals=0
        ),
        name="finish_swapped",
    )(parts, weight)


def place_kernel(core_ref, half_ref, delta_ref, video_ref, out_ref):
    out_ref[...] = (video_ref[...].astype(F32) + delta_ref[...].astype(F32)).astype(BF)


def place(core, half, delta, video):
    width = 768
    steps = D // 2 // width

    def other_place(step, core_ref):
        return (0, step + steps * (1 - core_ref[0]))

    return pl.pallas_call(
        place_kernel,
        grid_spec=pltpu.PrefetchScalarGridSpec(
            num_scalar_prefetch=1,
            grid=(steps,),
            in_specs=[
                pl.BlockSpec(memory_space=pl.ANY),
                pl.BlockSpec((SRC, width), lambda c, core_ref: (0, c)),
                pl.BlockSpec((SRC, width), other_place),
            ],
            out_specs=pl.BlockSpec((SRC, width), other_place),
        ),
        out_shape=jax.ShapeDtypeStruct((SRC, D), BF),
        input_output_aliases={1: 0},
        compiler_params=pltpu.CompilerParams(vmem_limit_bytes=16 << 20),
        name="place",
    )(core, half, delta, video)


SIZE = {"x": 4, "y": 4, "z": 8, "c": 2}


def shift(value, axis, by):
    size = SIZE[axis]
    return lax.ppermute(value, axis, [(i, (i + by) % size) for i in range(size)])


def cat(*pieces):
    return jnp.concatenate(pieces, axis=0)


def pick_kernel(core_ref, first_ref, second_ref, out_ref):
    @pl.when(core_ref[0] == 0)
    def _():
        out_ref[...] = first_ref[...]

    @pl.when(core_ref[0] != 0)
    def _():
        out_ref[...] = second_ref[...]


def pick(core, first, second):
    return pl.pallas_call(
        pick_kernel,
        in_specs=[
            pl.BlockSpec(memory_space=pltpu.SMEM),
            pl.BlockSpec(memory_space=pltpu.VMEM),
            pl.BlockSpec(memory_space=pltpu.VMEM),
        ],
        out_shape=jax.ShapeDtypeStruct(first.shape, first.dtype),
        compiler_params=pltpu.CompilerParams(vmem_limit_bytes=16 << 20),
        name="pick",
    )(core, first, second)


def far_shift(up, down, axis, core):
    size = SIZE[axis]
    pairs = []
    for i in range(size):
        pairs.append((2 * i, 2 * ((i + 1) % size)))
        pairs.append((2 * i + 1, 2 * ((i - 1) % size) + 1))
    return lax.ppermute(pick(core, up, down), (axis, "c"), pairs)


def gather_rows(a, b, core, project_set, later):
    a_near = [shift(a, "x", k) for k in (1, -1, 2)]
    b_near = [shift(b, "y", k) for k in (1, -1, 2)]
    a_line, b_line = join(a, *a_near), join(b, *b_near)
    around = [shift(a_line, "y", 1), shift(a_line, "y", -1)]
    around += [shift(b_line, "x", 1), shift(b_line, "x", -1)]
    near = project_set([a_line, b_line])
    near, around, later = lax.optimization_barrier((near, around, later))
    far = [far_shift(*around[:2], "y", core), far_shift(*around[2:], "x", core)]
    middle = project_set(around)
    return near, middle, project_set(far), later


def row_ids():
    x, y = lax.axis_index("x"), lax.axis_index("y")
    near = (0, -1, 1, 2)
    places = [(k, 0, 0) for k in near] + [(0, k, 1) for k in near]
    places += [(k, -1, 0) for k in near] + [(k, 1, 0) for k in near]
    places += [(-1, k, 1) for k in near] + [(1, k, 1) for k in near]
    places += [(k, 2, 0) for k in near] + [(2, k, 1) for k in near]
    dx, dy, part = (jnp.array(column, jnp.int32) for column in zip(*places))
    owner = (x + dx) % 4 * 4 + (y + dy) % 4
    half = MRG // 2
    ids = (owner * MRG + part * half)[:, None] + jnp.arange(half, dtype=jnp.int32)[None, :]
    return ids.reshape(1, ROWS).astype(F32)


def per_device(video, assign, qkv_weight, qk_gain, text_kv, out_weight):
    sq = ("x", "y")
    core = lax.axis_index("c").astype(jnp.int32)
    send = pack_rows(assign, video).reshape(SQ, CAP, WIDE)
    got = lax.all_to_all(send, sq, split_axis=0, concat_axis=0, tiled=True)
    low, high, need = merge_rows(got.reshape(SQ * CAP, WIDE))

    half_weight = lax.dynamic_slice_in_dim(out_weight, core * (D // 2), D // 2, 1)
    core = core.reshape(1)
    near, middle, far, half_weight = gather_rows(
        low, high, core, lambda rows: project(rows, qkv_weight, qk_gain), half_weight
    )
    own = lax.all_gather(half_weight, sq, axis=0, tiled=True)
    queries, kv = (cat(*pieces) for pieces in zip(near, middle, far))

    state = attend(queries, [kv], text=text_kv)
    swapped = [shift(kv, "c", 1)]
    up = down = kv
    for _ in range(3):
        up, down = shift(up, "z", 1), shift(down, "z", -1)
        state, up, down = lax.optimization_barrier((state, up, down))
        state = attend(queries, [up, down] + swapped, state)
        swapped = [shift(up, "c", 1), shift(down, "c", 1)]
    last = far_shift(up, down, "z", core)
    state, last = lax.optimization_barrier((state, last))
    state = attend(queries, [last] + swapped, state)
    swapped = [shift(last, "c", 1)]
    parts = attend(queries, swapped, state, finish_with=(need, row_ids()))
    parts = lax.all_to_all(parts, sq, split_axis=0, concat_axis=0, tiled=True)
    swapped = shift(parts, "c", 1)
    result, weight = finish_own(core, parts, own, video)
    swapped, weight = lax.optimization_barrier((swapped, weight))
    sent = shift(finish_swapped(swapped, weight), "c", 1)
    return place(core, result, sent, video)


def solution(mesh):
    fine = Mesh(mesh.devices.reshape(4, 4, 8, 2), ("x", "y", "z", "c"))
    sq = ("x", "y")
    in_specs = (
        P(("x", "y", "z", "c"), None),
        P(("x", "y", "z", "c")),
        P(None, sq),
        P(),
        P(None, None, sq),
        P(sq, None),
    )
    out_specs = P(("x", "y", "z", "c"), None)
    return jax.shard_map(
        per_device, mesh=fine, in_specs=in_specs, out_specs=out_specs, check_vma=False
    )
```

```python
import functools
import math

import jax
import jax.numpy as jnp
from jax import lax
from jax.experimental import pallas as pl
from jax.experimental.pallas import tpu as pltpu
from jax.sharding import Mesh, PartitionSpec as P

BF = jnp.bfloat16
F32 = jnp.float32
HD = 128
SQ = 16
SK = 16
CAP = 24
MRG = 48
SRC = 192
ROWS = SQ * MRG
TEXT = 256
D = 3072


def dot(a, b):
    return lax.dot_general(a, b, (((1,), (0,)), ((), ())), preferred_element_type=F32)


def dot_t(a, b):
    return lax.dot_general(a, b, (((1,), (1,)), ((), ())), preferred_element_type=F32)


WIDE = D + HD
HALF = SRC // 2


def pack_kernel(row_ref, video_ref, out_ref, tags_ref):
    row = row_ref[...]
    peer = row // (MRG * SK)
    local = row % MRG
    own_peer = lax.broadcasted_iota(jnp.int32, (SQ, SRC), 0) == peer
    hot = jnp.where(own_peer, 1.0, 0.0)
    before = lax.broadcasted_iota(jnp.int32, (SRC, SRC), 0) < lax.broadcasted_iota(
        jnp.int32, (SRC, SRC), 1
    )
    ranks = dot(hot.astype(BF), jnp.where(before, 1.0, 0.0).astype(BF))
    rank = jnp.sum(hot * ranks, axis=0, keepdims=True).astype(jnp.int32)
    position = peer * CAP + rank
    chosen = lax.broadcasted_iota(jnp.int32, (SQ * CAP, SRC), 0) == position
    out_ref[:, :D] = dot(jnp.where(chosen, 1.0, 0.0).astype(BF), video_ref[...]).astype(BF)
    number = (local + 1).astype(F32)
    slot_number = jnp.sum(jnp.where(chosen, number, 0.0), axis=1, keepdims=True)
    lanes = lax.broadcasted_iota(jnp.int32, (SQ * CAP, HD), 1)
    tags_ref[...] = jnp.where(lanes == HD - 1, slot_number, 0.0)
    for slot, part in enumerate((peer, local)):
        part = part.astype(F32)
        low, high = part[:, :HALF], part[:, HALF:]
        for place in range(2 * slot, SQ * CAP, CAP):
            tags_ref[place : place + 1, :HALF] = low
            tags_ref[place + 1 : place + 2, :HALF] = high
    out_ref[:, D:] = tags_ref[...].astype(BF)


def pack_rows(assign, video):
    return pl.pallas_call(
        pack_kernel,
        out_shape=jax.ShapeDtypeStruct((SQ * CAP, WIDE), BF),
        scratch_shapes=[pltpu.VMEM((SQ * CAP, HD), F32)],
        compiler_params=pltpu.CompilerParams(vmem_limit_bytes=16 << 20),
        name="pack_rows",
    )(assign.reshape(1, SRC), video)


def merge_kernel(got_ref, low_ref, high_ref, need_ref, tags_ref, flat_ref):
    tags_ref[...] = got_ref[:, D:].astype(F32)
    number = tags_ref[:, HD - 1 :]
    places = lax.broadcasted_iota(jnp.int32, (SQ * CAP, MRG), 1).astype(F32) + 1.0
    member = jnp.where(number == places, 1.0, 0.0).astype(BF)

    def over_slots(values):
        return lax.dot_general(
            member, values, (((0,), (0,)), ((), ())), preferred_element_type=F32
        )

    counts = over_slots(jnp.ones((SQ * CAP, HD), BF))[:, :1]
    merged = over_slots(got_ref[:, :D]) / jnp.maximum(counts, 1.0)
    low_ref[...] = merged[: MRG // 2].astype(BF)
    high_ref[...] = merged[MRG // 2 :].astype(BF)
    flat_ref[...] = jnp.zeros_like(flat_ref)
    for peer in range(SQ):
        for part in range(2):
            row = peer * CAP + part
            owner, local = tags_ref[row : row + 1, :HALF], tags_ref[row + 2 : row + 3, :HALF]
            flat_ref[peer : peer + 1, part * HALF : (part + 1) * HALF] = owner * MRG + local
    need_ref[...] = jnp.transpose(flat_ref[...])


def merge_rows(got):
    half = jax.ShapeDtypeStruct((MRG // 2, D), BF)
    return pl.pallas_call(
        merge_kernel,
        out_shape=[half, half, jax.ShapeDtypeStruct((2 * HD, HD), F32)],
        scratch_shapes=[pltpu.VMEM((SQ * CAP, HD), F32), pltpu.VMEM((HD, 2 * HD), F32)],
        compiler_params=pltpu.CompilerParams(vmem_limit_bytes=16 << 20),
        name="merge_rows",
    )(got)


def join_kernel(*refs):
    *parts, out_ref = refs
    out_ref[...] = jnp.concatenate([ref[...] for ref in parts], axis=0)


def join(*parts):
    rows = sum(part.shape[0] for part in parts)
    return pl.pallas_call(
        join_kernel,
        out_shape=jax.ShapeDtypeStruct((rows, parts[0].shape[1]), BF),
        compiler_params=pltpu.CompilerParams(vmem_limit_bytes=16 << 20),
        name="join",
    )(*parts)


def project_kernel(*refs):
    *row_refs, weight_ref, gain_ref, q_ref, kv_ref = refs

    def norm(part, gain):
        return part * lax.rsqrt(jnp.mean(part * part, axis=-1, keepdims=True) + 1e-06) * gain

    factor = math.log2(math.e) / math.sqrt(HD)
    full = dot(jnp.concatenate([ref[...] for ref in row_refs], axis=0), weight_ref[...])
    q_ref[...] = (norm(full[:, :HD], gain_ref[0:1, :]) * factor).astype(BF)
    kv_ref[:, :HD] = norm(full[:, HD : 2 * HD], gain_ref[1:2, :]).astype(BF)
    kv_ref[:, HD:] = full[:, 2 * HD :].astype(BF)


def project(pieces, weight, gain):
    count = sum(piece.shape[0] for piece in pieces)
    return pl.pallas_call(
        project_kernel,
        out_shape=[
            jax.ShapeDtypeStruct((count, HD), BF),
            jax.ShapeDtypeStruct((count, 2 * HD), BF),
        ],
        compiler_params=pltpu.CompilerParams(vmem_limit_bytes=16 << 20),
        cost_estimate=pl.CostEstimate(
            flops=2 * count * D * 3 * HD, bytes_accessed=2 * D * (count + 3 * HD), transcendentals=0
        ),
        name="project",
    )(*pieces, weight, gain)


QB = 256
CHUNK = 768


def attend_kernel(first, last, pieces, *refs):
    q_ref, *refs = refs
    text_ref = refs.pop(0) if first else None
    kv_refs = [refs.pop(0) for _ in range(pieces)]
    if not first:
        m_in, acc_in = refs.pop(0), refs.pop(0)
    if last:
        need_ref, ids_ref, out_ref, m_ref, acc_ref, wide_ref, done_ref = refs
    else:
        m_ref, acc_ref, wide_ref = refs

    wide_ref[:, HD:] = jnp.ones((wide_ref.shape[0], HD), BF)
    chunks = []
    place = 0
    if first:
        wide_ref[:TEXT, :HD] = text_ref[1]
        chunks.append((text_ref[0], 0, TEXT))
        place = TEXT
    for ref in kv_refs:
        size = ref.shape[0]
        wide_ref[place : place + size, :HD] = ref[:, HD:]
        for start in range(0, size, CHUNK):
            width = min(CHUNK, size - start)
            chunks.append((ref[start : start + width, :HD], place + start, width))
        place += size

    for index, (keys, start, width) in enumerate(chunks):
        values = wide_ref[start : start + width, :]
        fresh = first and index == 0
        from_m, from_acc = (m_in, acc_in) if index == 0 and not first else (m_ref, acc_ref)
        for block in range(ROWS // QB):
            span = pl.ds(block * QB, QB)
            scores = dot_t(q_ref[span, :], keys)
            raised = jnp.max(scores, axis=-1, keepdims=True)
            if not fresh:
                before = from_m[span, :1]
                raised = jnp.maximum(before, raised)
                fading = jnp.exp2(before - raised)
            probs = jnp.exp2(scores - raised).astype(BF)
            update = dot(probs, values)
            if not fresh:
                update = from_acc[span, :] * fading + update
            acc_ref[span, :] = update
            m_ref[span, :] = jnp.broadcast_to(raised, (QB, HD))

    if last:
        done_ref[...] = (acc_ref[:, :HD] / acc_ref[:, HD:]).astype(BF)
        for peer in range(SQ):
            wanted = need_ref[:SRC, peer : peer + 1]
            hot = jnp.where(wanted == ids_ref[...], 1.0, 0.0).astype(BF)
            out_ref[peer] = dot(hot, done_ref[...]).astype(BF)


def attend(queries, kv, state=None, text=None, finish_with=None):
    first, last = text is not None, finish_with is not None
    keys = sum(piece.shape[0] for piece in kv) + (TEXT if first else 0)
    shapes = [(ROWS, HD), (ROWS, 2 * HD)]
    scratch = [pltpu.VMEM((keys, 2 * HD), BF)]
    operands = [queries] + ([text] if first else []) + list(kv) + ([] if first else list(state))
    if last:
        operands += list(finish_with)
        out_shape = jax.ShapeDtypeStruct((SQ, SRC, HD), BF)
        scratch = [pltpu.VMEM(shape, F32) for shape in shapes] + scratch
        scratch.append(pltpu.VMEM((ROWS, HD), BF))
    else:
        out_shape = [jax.ShapeDtypeStruct(shape, F32) for shape in shapes]
    return pl.pallas_call(
        functools.partial(attend_kernel, first, last, len(kv)),
        out_shape=out_shape,
        input_output_aliases={} if first or last else {len(kv) + 1: 0, len(kv) + 2: 1},
        scratch_shapes=scratch,
        compiler_params=pltpu.CompilerParams(vmem_limit_bytes=16 << 20),
        cost_estimate=pl.CostEstimate(
            flops=6 * ROWS * keys * HD,
            bytes_accessed=4 * keys * HD,
            transcendentals=ROWS * keys,
        ),
        name="attend",
    )(*operands)


STRIPS = 8


def load_kernel(weight_hbm, weight_ref, sems):
    rows = SQ * HD // STRIPS
    copies = []
    for strip in range(STRIPS):
        span = pl.ds(strip * rows, rows)
        copies.append(
            pltpu.make_async_copy(weight_hbm.at[span], weight_ref.at[span], sems.at[strip])
        )
    for copy in copies:
        copy.start()
    for copy in copies:
        copy.wait()


def load(weight):
    return pl.pallas_call(
        load_kernel,
        in_specs=[pl.BlockSpec(memory_space=pltpu.HBM)],
        out_specs=pl.BlockSpec(memory_space=pltpu.VMEM),
        out_shape=pltpu.VMEM(weight.shape, BF),
        scratch_shapes=[pltpu.SemaphoreType.DMA((STRIPS,))],
        compiler_params=pltpu.CompilerParams(vmem_limit_bytes=44 << 20),
        cost_estimate=pl.CostEstimate(
            flops=0, bytes_accessed=2 * weight.size, transcendentals=0
        ),
        name="load",
    )(weight)


def half_columns(index):
    return pl.ds(pl.multiple_of(index * (D // 2), D // 2), D // 2)


def half_update(parts_ref, weight_ref, flat_ref):
    for group in range(SQ):
        flat_ref[:, group * HD : (group + 1) * HD] = parts_ref[group]
    return dot(flat_ref[...], weight_ref[...]).astype(BF)


PRODUCT = pl.CostEstimate(
    flops=SRC * SQ * HD * D, bytes_accessed=SQ * HD * D, transcendentals=0
)


def own_kernel(core_ref, parts_ref, weight_ref, video_ref, out_ref, flat_ref):
    columns = half_columns(core_ref[0])
    delta = half_update(parts_ref, weight_ref, flat_ref).astype(F32)
    out_ref[:, columns] = (video_ref[:, columns].astype(F32) + delta).astype(BF)


def finish_own(core, parts, weight, video):
    vmem = pl.BlockSpec(memory_space=pltpu.VMEM)
    return pl.pallas_call(
        own_kernel,
        in_specs=[pl.BlockSpec(memory_space=pltpu.SMEM), vmem, vmem, vmem],
        out_shape=jax.ShapeDtypeStruct((SRC, D), BF),
        scratch_shapes=[pltpu.VMEM((SRC, SQ * HD), BF)],
        compiler_params=pltpu.CompilerParams(vmem_limit_bytes=20 << 20),
        cost_estimate=PRODUCT,
        name="finish_own",
    )(core, parts, weight, video)


def swapped_kernel(parts_ref, weight_ref, out_ref, flat_ref):
    out_ref[...] = half_update(parts_ref, weight_ref, flat_ref)


def finish_swapped(parts, weight):
    return pl.pallas_call(
        swapped_kernel,
        out_shape=jax.ShapeDtypeStruct((SRC, D // 2), BF),
        scratch_shapes=[pltpu.VMEM((SRC, SQ * HD), BF)],
        compiler_params=pltpu.CompilerParams(vmem_limit_bytes=20 << 20),
        cost_estimate=PRODUCT,
        name="finish_swapped",
    )(parts, weight)


def place_kernel(core_ref, half_ref, delta_ref, video_ref, out_ref):
    out_ref[...] = (video_ref[...].astype(F32) + delta_ref[...].astype(F32)).astype(BF)


def place(core, half, delta, video):
    width = 768
    steps = D // 2 // width

    def other_place(step, core_ref):
        return (0, step + steps * (1 - core_ref[0]))

    return pl.pallas_call(
        place_kernel,
        grid_spec=pltpu.PrefetchScalarGridSpec(
            num_scalar_prefetch=1,
            grid=(steps,),
            in_specs=[
                pl.BlockSpec(memory_space=pl.ANY),
                pl.BlockSpec((SRC, width), lambda c, core_ref: (0, c)),
                pl.BlockSpec((SRC, width), other_place),
            ],
            out_specs=pl.BlockSpec((SRC, width), other_place),
        ),
        out_shape=jax.ShapeDtypeStruct((SRC, D), BF),
        input_output_aliases={1: 0},
        compiler_params=pltpu.CompilerParams(vmem_limit_bytes=16 << 20),
        name="place",
    )(core, half, delta, video)


SIZE = {"x": 4, "y": 4, "z": 8, "c": 2}


def shift(value, axis, by):
    size = SIZE[axis]
    return lax.ppermute(value, axis, [(i, (i + by) % size) for i in range(size)])


def cat(*pieces):
    return jnp.concatenate(pieces, axis=0)


def pick_kernel(core_ref, first_ref, second_ref, out_ref, sem):
    def bring(source):
        copy = pltpu.make_async_copy(source, out_ref, sem)
        copy.start()
        copy.wait()

    @pl.when(core_ref[0] == 0)
    def _():
        bring(first_ref)

    @pl.when(core_ref[0] != 0)
    def _():
        bring(second_ref)


def pick(core, first, second):
    anywhere = pl.BlockSpec(memory_space=pl.ANY)
    return pl.pallas_call(
        pick_kernel,
        in_specs=[pl.BlockSpec(memory_space=pltpu.SMEM), anywhere, anywhere],
        out_specs=anywhere,
        out_shape=jax.ShapeDtypeStruct(first.shape, first.dtype),
        scratch_shapes=[pltpu.SemaphoreType.DMA],
        compiler_params=pltpu.CompilerParams(vmem_limit_bytes=16 << 20),
        name="pick",
    )(core, first, second)


def far_shift(up, down, axis, core):
    size = SIZE[axis]
    pairs = []
    for i in range(size):
        pairs.append((2 * i, 2 * ((i + 1) % size)))
        pairs.append((2 * i + 1, 2 * ((i - 1) % size) + 1))
    return lax.ppermute(pick(core, up, down), (axis, "c"), pairs)


def gather_rows(a, b, core, project_set, later):
    a_near = [shift(a, "x", k) for k in (1, -1, 2)]
    b_near = [shift(b, "y", k) for k in (1, -1, 2)]
    a_line, b_line = join(a, *a_near), join(b, *b_near)
    around = [shift(a_line, "y", 1), shift(a_line, "y", -1)]
    around += [shift(b_line, "x", 1), shift(b_line, "x", -1)]
    near = project_set([a_line, b_line])
    near, around, later = lax.optimization_barrier((near, around, later))
    far = [far_shift(*around[:2], "y", core), far_shift(*around[2:], "x", core)]
    middle = project_set(around)
    return near, middle, project_set(far), later


def row_ids():
    x, y = lax.axis_index("x"), lax.axis_index("y")
    near = (0, -1, 1, 2)
    places = [(k, 0, 0) for k in near] + [(0, k, 1) for k in near]
    places += [(k, -1, 0) for k in near] + [(k, 1, 0) for k in near]
    places += [(-1, k, 1) for k in near] + [(1, k, 1) for k in near]
    places += [(k, 2, 0) for k in near] + [(2, k, 1) for k in near]
    dx, dy, part = (jnp.array(column, jnp.int32) for column in zip(*places))
    owner = (x + dx) % 4 * 4 + (y + dy) % 4
    half = MRG // 2
    ids = (owner * MRG + part * half)[:, None] + jnp.arange(half, dtype=jnp.int32)[None, :]
    return ids.reshape(1, ROWS).astype(F32)


def per_device(video, assign, qkv_weight, qk_gain, text_kv, out_weight):
    sq = ("x", "y")
    core = lax.axis_index("c").astype(jnp.int32)
    send = pack_rows(assign, video).reshape(SQ, CAP, WIDE)
    got = lax.all_to_all(send, sq, split_axis=0, concat_axis=0, tiled=True)
    low, high, need = merge_rows(got.reshape(SQ * CAP, WIDE))

    half_weight = lax.dynamic_slice_in_dim(out_weight, core * (D // 2), D // 2, 1)
    core = core.reshape(1)
    near, middle, far, half_weight = gather_rows(
        low, high, core, lambda rows: project(rows, qkv_weight, qk_gain), half_weight
    )
    own = lax.all_gather(half_weight, sq, axis=0, tiled=True)
    queries, kv = (cat(*pieces) for pieces in zip(near, middle, far))

    state = attend(queries, [kv], text=text_kv)
    swapped = [shift(kv, "c", 1)]
    up = down = kv
    for _ in range(3):
        up, down = shift(up, "z", 1), shift(down, "z", -1)
        state, up, down = lax.optimization_barrier((state, up, down))
        state = attend(queries, [up, down] + swapped, state)
        swapped = [shift(up, "c", 1), shift(down, "c", 1)]
    last = far_shift(up, down, "z", core)
    state, last = lax.optimization_barrier((state, last))
    state = attend(queries, [last] + swapped, state)
    swapped = [shift(last, "c", 1)]
    parts = attend(queries, swapped, state, finish_with=(need, row_ids()))
    parts = lax.all_to_all(parts, sq, split_axis=0, concat_axis=0, tiled=True)
    swapped = shift(parts, "c", 1)
    weight = load(own)
    swapped, weight, parts = lax.optimization_barrier((swapped, weight, parts))
    sent = finish_swapped(swapped, weight)
    sent, weight, parts = lax.optimization_barrier((sent, weight, parts))
    delta = shift(sent, "c", 1)
    result = finish_own(core, parts, weight, video)
    return place(core, result, delta, video)


def solution(mesh):
    fine = Mesh(mesh.devices.reshape(4, 4, 8, 2), ("x", "y", "z", "c"))
    sq = ("x", "y")
    in_specs = (
        P(("x", "y", "z", "c"), None),
        P(("x", "y", "z", "c")),
        P(None, sq),
        P(),
        P(None, None, sq),
        P(sq, None),
    )
    out_specs = P(("x", "y", "z", "c"), None)
    return jax.shard_map(
        per_device, mesh=fine, in_specs=in_specs, out_specs=out_specs, check_vma=False
    )
```

```python
import functools
import math

import jax
import jax.numpy as jnp
from jax import lax
from jax.experimental import pallas as pl
from jax.experimental.pallas import tpu as pltpu
from jax.sharding import Mesh, PartitionSpec as P

BF = jnp.bfloat16
F32 = jnp.float32
HD = 128
SQ = 16
SK = 16
CAP = 24
MRG = 48
SRC = 192
ROWS = SQ * MRG
TEXT = 256
D = 3072


def dot(a, b):
    return lax.dot_general(a, b, (((1,), (0,)), ((), ())), preferred_element_type=F32)


def dot_t(a, b):
    return lax.dot_general(a, b, (((1,), (1,)), ((), ())), preferred_element_type=F32)


WIDE = D + HD
HALF = SRC // 2


def pack_kernel(row_ref, video_ref, out_ref, tags_ref):
    row = row_ref[...]
    peer = row // (MRG * SK)
    local = row % MRG
    own_peer = lax.broadcasted_iota(jnp.int32, (SQ, SRC), 0) == peer
    hot = jnp.where(own_peer, 1.0, 0.0)
    before = lax.broadcasted_iota(jnp.int32, (SRC, SRC), 0) < lax.broadcasted_iota(
        jnp.int32, (SRC, SRC), 1
    )
    ranks = dot(hot.astype(BF), jnp.where(before, 1.0, 0.0).astype(BF))
    rank = jnp.sum(hot * ranks, axis=0, keepdims=True).astype(jnp.int32)
    position = peer * CAP + rank
    chosen = lax.broadcasted_iota(jnp.int32, (SQ * CAP, SRC), 0) == position
    out_ref[:, :D] = dot(jnp.where(chosen, 1.0, 0.0).astype(BF), video_ref[...]).astype(BF)
    number = (local + 1).astype(F32)
    slot_number = jnp.sum(jnp.where(chosen, number, 0.0), axis=1, keepdims=True)
    lanes = lax.broadcasted_iota(jnp.int32, (SQ * CAP, HD), 1)
    tags_ref[...] = jnp.where(lanes == HD - 1, slot_number, 0.0)
    for slot, part in enumerate((peer, local)):
        part = part.astype(F32)
        low, high = part[:, :HALF], part[:, HALF:]
        for place in range(2 * slot, SQ * CAP, CAP):
            tags_ref[place : place + 1, :HALF] = low
            tags_ref[place + 1 : place + 2, :HALF] = high
    out_ref[:, D:] = tags_ref[...].astype(BF)


def pack_rows(assign, video):
    return pl.pallas_call(
        pack_kernel,
        out_shape=jax.ShapeDtypeStruct((SQ * CAP, WIDE), BF),
        scratch_shapes=[pltpu.VMEM((SQ * CAP, HD), F32)],
        compiler_params=pltpu.CompilerParams(vmem_limit_bytes=16 << 20),
        name="pack_rows",
    )(assign.reshape(1, SRC), video)


def merge_kernel(got_ref, low_ref, high_ref, need_ref, tags_ref, flat_ref):
    tags_ref[...] = got_ref[:, D:].astype(F32)
    number = tags_ref[:, HD - 1 :]
    places = lax.broadcasted_iota(jnp.int32, (SQ * CAP, MRG), 1).astype(F32) + 1.0
    member = jnp.where(number == places, 1.0, 0.0).astype(BF)

    def over_slots(values):
        return lax.dot_general(
            member, values, (((0,), (0,)), ((), ())), preferred_element_type=F32
        )

    counts = over_slots(jnp.ones((SQ * CAP, HD), BF))[:, :1]
    merged = over_slots(got_ref[:, :D]) / jnp.maximum(counts, 1.0)
    low_ref[...] = merged[: MRG // 2].astype(BF)
    high_ref[...] = merged[MRG // 2 :].astype(BF)
    flat_ref[...] = jnp.zeros_like(flat_ref)
    for peer in range(SQ):
        for part in range(2):
            row = peer * CAP + part
            owner, local = tags_ref[row : row + 1, :HALF], tags_ref[row + 2 : row + 3, :HALF]
            flat_ref[peer : peer + 1, part * HALF : (part + 1) * HALF] = owner * MRG + local
    need_ref[...] = jnp.transpose(flat_ref[...])


def merge_rows(got):
    half = jax.ShapeDtypeStruct((MRG // 2, D), BF)
    return pl.pallas_call(
        merge_kernel,
        out_shape=[half, half, jax.ShapeDtypeStruct((2 * HD, HD), F32)],
        scratch_shapes=[pltpu.VMEM((SQ * CAP, HD), F32), pltpu.VMEM((HD, 2 * HD), F32)],
        compiler_params=pltpu.CompilerParams(vmem_limit_bytes=16 << 20),
        name="merge_rows",
    )(got)


def join_kernel(*refs):
    *parts, out_ref = refs
    out_ref[...] = jnp.concatenate([ref[...] for ref in parts], axis=0)


def join(*parts):
    rows = sum(part.shape[0] for part in parts)
    return pl.pallas_call(
        join_kernel,
        out_shape=jax.ShapeDtypeStruct((rows, parts[0].shape[1]), BF),
        compiler_params=pltpu.CompilerParams(vmem_limit_bytes=16 << 20),
        name="join",
    )(*parts)


def project_kernel(*refs):
    *row_refs, weight_ref, gain_ref, q_ref, kv_ref = refs

    def norm(part, gain):
        return part * lax.rsqrt(jnp.mean(part * part, axis=-1, keepdims=True) + 1e-06) * gain

    factor = math.log2(math.e) / math.sqrt(HD)
    full = dot(jnp.concatenate([ref[...] for ref in row_refs], axis=0), weight_ref[...])
    q_ref[...] = (norm(full[:, :HD], gain_ref[0:1, :]) * factor).astype(BF)
    kv_ref[:, :HD] = norm(full[:, HD : 2 * HD], gain_ref[1:2, :]).astype(BF)
    kv_ref[:, HD:] = full[:, 2 * HD :].astype(BF)


def project(pieces, weight, gain):
    count = sum(piece.shape[0] for piece in pieces)
    return pl.pallas_call(
        project_kernel,
        out_shape=[
            jax.ShapeDtypeStruct((count, HD), BF),
            jax.ShapeDtypeStruct((count, 2 * HD), BF),
        ],
        compiler_params=pltpu.CompilerParams(vmem_limit_bytes=16 << 20),
        cost_estimate=pl.CostEstimate(
            flops=2 * count * D * 3 * HD, bytes_accessed=2 * D * (count + 3 * HD), transcendentals=0
        ),
        name="project",
    )(*pieces, weight, gain)


QB = 256
CHUNK = 768


def attend_kernel(first, last, pieces, *refs):
    q_ref, *refs = refs
    text_ref = refs.pop(0) if first else None
    kv_refs = [refs.pop(0) for _ in range(pieces)]
    if not first:
        m_in, acc_in = refs.pop(0), refs.pop(0)
    if last:
        need_ref, ids_ref, out_ref, m_ref, acc_ref, wide_ref, done_ref = refs
    else:
        m_ref, acc_ref, wide_ref = refs

    wide_ref[:, HD:] = jnp.ones((wide_ref.shape[0], HD), BF)
    chunks = []
    place = 0
    if first:
        wide_ref[:TEXT, :HD] = text_ref[1]
        chunks.append((text_ref[0], 0, TEXT))
        place = TEXT
    for ref in kv_refs:
        size = ref.shape[0]
        wide_ref[place : place + size, :HD] = ref[:, HD:]
        for start in range(0, size, CHUNK):
            width = min(CHUNK, size - start)
            chunks.append((ref[start : start + width, :HD], place + start, width))
        place += size

    for index, (keys, start, width) in enumerate(chunks):
        values = wide_ref[start : start + width, :]
        fresh = first and index == 0
        from_m, from_acc = (m_in, acc_in) if index == 0 and not first else (m_ref, acc_ref)
        for block in range(ROWS // QB):
            span = pl.ds(block * QB, QB)
            scores = dot_t(q_ref[span, :], keys)
            raised = jnp.max(scores, axis=-1, keepdims=True)
            if not fresh:
                before = from_m[span, :1]
                raised = jnp.maximum(before, raised)
                fading = jnp.exp2(before - raised)
            probs = jnp.exp2(scores - raised).astype(BF)
            update = dot(probs, values)
            if not fresh:
                update = from_acc[span, :] * fading + update
            acc_ref[span, :] = update
            m_ref[span, :] = jnp.broadcast_to(raised, (QB, HD))

    if last:
        done_ref[...] = (acc_ref[:, :HD] / acc_ref[:, HD:]).astype(BF)
        for peer in range(SQ):
            wanted = need_ref[:SRC, peer : peer + 1]
            hot = jnp.where(wanted == ids_ref[...], 1.0, 0.0).astype(BF)
            out_ref[peer] = dot(hot, done_ref[...]).astype(BF)


def attend(queries, kv, state=None, text=None, finish_with=None):
    first, last = text is not None, finish_with is not None
    keys = sum(piece.shape[0] for piece in kv) + (TEXT if first else 0)
    shapes = [(ROWS, HD), (ROWS, 2 * HD)]
    scratch = [pltpu.VMEM((keys, 2 * HD), BF)]
    operands = [queries] + ([text] if first else []) + list(kv) + ([] if first else list(state))
    if last:
        operands += list(finish_with)
        out_shape = jax.ShapeDtypeStruct((SQ, SRC, HD), BF)
        scratch = [pltpu.VMEM(shape, F32) for shape in shapes] + scratch
        scratch.append(pltpu.VMEM((ROWS, HD), BF))
    else:
        out_shape = [jax.ShapeDtypeStruct(shape, F32) for shape in shapes]
    return pl.pallas_call(
        functools.partial(attend_kernel, first, last, len(kv)),
        out_shape=out_shape,
        input_output_aliases={} if first or last else {len(kv) + 1: 0, len(kv) + 2: 1},
        scratch_shapes=scratch,
        compiler_params=pltpu.CompilerParams(vmem_limit_bytes=16 << 20),
        cost_estimate=pl.CostEstimate(
            flops=6 * ROWS * keys * HD,
            bytes_accessed=4 * keys * HD,
            transcendentals=ROWS * keys,
        ),
        name="attend",
    )(*operands)


STRIPS = 8


def load_kernel(weight_hbm, weight_ref, sems):
    rows = SQ * HD // STRIPS
    copies = []
    for strip in range(STRIPS):
        span = pl.ds(strip * rows, rows)
        copies.append(
            pltpu.make_async_copy(weight_hbm.at[span], weight_ref.at[span], sems.at[strip])
        )
    for copy in copies:
        copy.start()
    for copy in copies:
        copy.wait()


def load(weight):
    return pl.pallas_call(
        load_kernel,
        in_specs=[pl.BlockSpec(memory_space=pltpu.HBM)],
        out_specs=pl.BlockSpec(memory_space=pltpu.VMEM),
        out_shape=pltpu.VMEM(weight.shape, BF),
        scratch_shapes=[pltpu.SemaphoreType.DMA((STRIPS,))],
        compiler_params=pltpu.CompilerParams(vmem_limit_bytes=44 << 20),
        cost_estimate=pl.CostEstimate(
            flops=0, bytes_accessed=2 * weight.size, transcendentals=0
        ),
        name="load",
    )(weight)


def half_update(parts_ref, weight_ref, flat_ref):
    for group in range(SQ):
        flat_ref[:, group * HD : (group + 1) * HD] = parts_ref[group]
    return dot(flat_ref[...], weight_ref[...]).astype(BF)


PRODUCT = pl.CostEstimate(
    flops=SRC * SQ * HD * D, bytes_accessed=SQ * HD * D, transcendentals=0
)


def own_kernel(core_ref, parts_ref, weight_ref, video_ref, out_ref, flat_ref):
    delta = half_update(parts_ref, weight_ref, flat_ref).astype(F32)
    out_ref[...] = (video_ref[...].astype(F32) + delta).astype(BF)


def finish_own(core, parts, weight, video):
    vmem = pl.BlockSpec(memory_space=pltpu.VMEM)
    columns = pl.BlockSpec((SRC, D // 2), lambda step, core_ref: (0, core_ref[0]))
    return pl.pallas_call(
        own_kernel,
        grid_spec=pltpu.PrefetchScalarGridSpec(
            num_scalar_prefetch=1,
            grid=(1,),
            in_specs=[vmem, vmem, columns],
            out_specs=columns,
            scratch_shapes=[pltpu.VMEM((SRC, SQ * HD), BF)],
        ),
        out_shape=jax.ShapeDtypeStruct((SRC, D), BF),
        compiler_params=pltpu.CompilerParams(vmem_limit_bytes=20 << 20),
        cost_estimate=PRODUCT,
        name="finish_own",
    )(core, parts, weight, video)


def swapped_kernel(parts_ref, weight_ref, out_ref, flat_ref):
    out_ref[...] = half_update(parts_ref, weight_ref, flat_ref)


def finish_swapped(parts, weight):
    return pl.pallas_call(
        swapped_kernel,
        out_shape=jax.ShapeDtypeStruct((SRC, D // 2), BF),
        scratch_shapes=[pltpu.VMEM((SRC, SQ * HD), BF)],
        compiler_params=pltpu.CompilerParams(vmem_limit_bytes=20 << 20),
        cost_estimate=PRODUCT,
        name="finish_swapped",
    )(parts, weight)


def place_kernel(core_ref, half_ref, delta_ref, video_ref, out_ref):
    out_ref[...] = (video_ref[...].astype(F32) + delta_ref[...].astype(F32)).astype(BF)


def place(core, half, delta, video):
    width = 768
    steps = D // 2 // width

    def other_place(step, core_ref):
        return (0, step + steps * (1 - core_ref[0]))

    return pl.pallas_call(
        place_kernel,
        grid_spec=pltpu.PrefetchScalarGridSpec(
            num_scalar_prefetch=1,
            grid=(steps,),
            in_specs=[
                pl.BlockSpec(memory_space=pl.ANY),
                pl.BlockSpec((SRC, width), lambda c, core_ref: (0, c)),
                pl.BlockSpec((SRC, width), other_place),
            ],
            out_specs=pl.BlockSpec((SRC, width), other_place),
        ),
        out_shape=jax.ShapeDtypeStruct((SRC, D), BF),
        input_output_aliases={1: 0},
        compiler_params=pltpu.CompilerParams(vmem_limit_bytes=16 << 20),
        name="place",
    )(core, half, delta, video)


SIZE = {"x": 4, "y": 4, "z": 8, "c": 2}


def shift(value, axis, by):
    size = SIZE[axis]
    return lax.ppermute(value, axis, [(i, (i + by) % size) for i in range(size)])


def cat(*pieces):
    return jnp.concatenate(pieces, axis=0)


def pick_kernel(core_ref, first_ref, second_ref, out_ref, sem):
    def bring(source):
        copy = pltpu.make_async_copy(source, out_ref, sem)
        copy.start()
        copy.wait()

    @pl.when(core_ref[0] == 0)
    def _():
        bring(first_ref)

    @pl.when(core_ref[0] != 0)
    def _():
        bring(second_ref)


def pick(core, first, second):
    anywhere = pl.BlockSpec(memory_space=pl.ANY)
    return pl.pallas_call(
        pick_kernel,
        in_specs=[pl.BlockSpec(memory_space=pltpu.SMEM), anywhere, anywhere],
        out_specs=anywhere,
        out_shape=jax.ShapeDtypeStruct(first.shape, first.dtype),
        scratch_shapes=[pltpu.SemaphoreType.DMA],
        compiler_params=pltpu.CompilerParams(vmem_limit_bytes=16 << 20),
        name="pick",
    )(core, first, second)


def twin_shift(value, axis, by):
    size = SIZE[axis]
    pairs = []
    for i in range(size):
        pairs.append((2 * i, 2 * ((i + by) % size)))
        pairs.append((2 * i + 1, 2 * ((i - by) % size) + 1))
    return lax.ppermute(value, (axis, "c"), pairs)


def gather_rows(a, b, project_set, later):
    a_near = [shift(a, "x", k) for k in (1, -1, 2)]
    b_near = [shift(b, "y", k) for k in (1, -1, 2)]
    a_line, b_line = join(a, *a_near), join(b, *b_near)
    around = [twin_shift(a_line, "y", 1), twin_shift(a_line, "y", -1)]
    around += [twin_shift(b_line, "x", 1), twin_shift(b_line, "x", -1)]
    near = project_set([a_line, b_line])
    near, around, later = lax.optimization_barrier((near, around, later))
    far = [twin_shift(around[0], "y", 1), twin_shift(around[2], "x", 1)]
    middle = project_set(around)
    return near, middle, project_set(far), later


def row_ids(core):
    x, y = lax.axis_index("x"), lax.axis_index("y")
    side = 2 * core - 1
    near = (0, -1, 1, 2)
    places = [(k, 0, 0) for k in near] + [(0, k, 1) for k in near]
    places += [(k, side, 0) for k in near] + [(k, -side, 0) for k in near]
    places += [(side, k, 1) for k in near] + [(-side, k, 1) for k in near]
    places += [(k, 2, 0) for k in near] + [(2, k, 1) for k in near]
    owners = [(x + dx) % 4 * 4 + (y + dy) % 4 for dx, dy, _ in places]
    half = MRG // 2
    starts = [owner * MRG + part * half for owner, (_, _, part) in zip(owners, places)]
    ids = jnp.stack(starts)[:, None] + jnp.arange(half, dtype=jnp.int32)[None, :]
    return ids.reshape(1, ROWS).astype(F32)


def per_device(video, assign, qkv_weight, qk_gain, text_kv, out_weight):
    sq = ("x", "y")
    core = lax.axis_index("c").astype(jnp.int32)
    send = pack_rows(assign, video).reshape(SQ, CAP, WIDE)
    got = lax.all_to_all(send, sq, split_axis=0, concat_axis=0, tiled=True)
    low, high, need = merge_rows(got.reshape(SQ * CAP, WIDE))

    half_weight = lax.dynamic_slice_in_dim(out_weight, core * (D // 2), D // 2, 1)
    core = core.reshape(1)
    near, middle, far, half_weight = gather_rows(
        low, high, lambda rows: project(rows, qkv_weight, qk_gain), half_weight
    )
    own = lax.all_gather(half_weight, sq, axis=0, tiled=True)
    queries, kv = (cat(*pieces) for pieces in zip(near, middle, far))

    state = attend(queries, [kv], text=text_kv)
    swapped = [shift(kv, "c", 1)]
    up = down = kv
    for _ in range(3):
        up, down = shift(up, "z", 1), shift(down, "z", -1)
        state, up, down = lax.optimization_barrier((state, up, down))
        state = attend(queries, [up, down] + swapped, state)
        swapped = [shift(up, "c", 1), shift(down, "c", 1)]
    last = twin_shift(pick(core, up, down), "z", 1)
    state, last = lax.optimization_barrier((state, last))
    state = attend(queries, [last] + swapped, state)
    swapped = [shift(last, "c", 1)]
    parts = attend(queries, swapped, state, finish_with=(need, row_ids(core[0])))
    parts = lax.all_to_all(parts, sq, split_axis=0, concat_axis=0, tiled=True)
    swapped = shift(parts, "c", 1)
    weight = load(own)
    swapped, weight, parts = lax.optimization_barrier((swapped, weight, parts))
    sent = finish_swapped(swapped, weight)
    sent, weight, parts = lax.optimization_barrier((sent, weight, parts))
    delta = shift(sent, "c", 1)
    result = finish_own(core, parts, weight, video)
    return place(core, result, delta, video)


def solution(mesh):
    fine = Mesh(mesh.devices.reshape(4, 4, 8, 2), ("x", "y", "z", "c"))
    sq = ("x", "y")
    in_specs = (
        P(("x", "y", "z", "c"), None),
        P(("x", "y", "z", "c")),
        P(None, sq),
        P(),
        P(None, None, sq),
        P(sq, None),
    )
    out_specs = P(("x", "y", "z", "c"), None)
    return jax.shard_map(
        per_device, mesh=fine, in_specs=in_specs, out_specs=out_specs, check_vma=False
    )
```
